256 devices in a mesh: dp: 32 (over x, y, core), rep: 8 (over z).
Axes of the slice: x: 4, y: 4, z: 8, core: 2. Of those that a mesh axis runs over, the one named last changes fastest.
Arguments:
- cache: bfloat16 [2048, 64, 576], P(('rep', 'dp')), parts along dimension 0, may hold values from -6 to 6
- lengths: int32 [2048], P(('rep', 'dp')), parts along dimension 0, may hold values from 2 to 62
- queries: bfloat16 [2048, 2, 64, 576], P(('rep', 'dp')), parts along dimension 0, may hold values from -4 to 4
- fresh: bfloat16 [2048, 2, 576], P(('rep', 'dp')), parts along dimension 0, may hold values from -6 to 6
- w_uv: bfloat16 [64, 512, 128], P('dp'), may hold values from -0.25 to 0.25
- w_out: bfloat16 [8192, 7168], P('dp'), may hold values from -0.0625 to 0.0625
- outgoing: int32 [1024], P(('rep', 'dp')), parts along dimension 0, may hold values from 0 to 7, as said below
- targets: int32 [1024], P(('rep', 'dp')), parts along dimension 0, may hold values from 0 to 31, as said below
Outputs:
- new_cache: bfloat16 [2048, 64, 576], P(('rep', 'dp')), parts along dimension 0
- attended: bfloat16 [2048, 2, 7168], P(('rep', 'dp')), parts along dimension 0
The draws below stay inside these ranges and needn't reach their ends.
There are 8 independent parts, one for each index of `rep`. The reference program is written for one: setup_inputs(seed, part) draws one part's arguments, and reference() takes and returns one part's arrays. A program takes and returns all parts, laid end to end along the dimension named above; an argument that names none is the same for every part. Nothing has to cross between parts.
Inputs may be any that keep to these rules, and one draw needn't show every extreme that they name: `outgoing`: the 4 slots listed for one device are different. `targets`: the 4 rows of one device go to 4 different other devices, and every device receives exactly 4 rows.
All inputs are finite; a program needn't handle non-finite values.
Results may differ from the reference program's by a relative error of at most 0.019.
Values may be sent and summed in bfloat16 or wider, within the bound.
A program may use at most 64 MiB of HBM per device.

```python
import math
import jax
import jax.numpy as jnp
from jax import lax

D = 7168
H = 64
LAT = 512
ROPE = 64
VD = 128
STEPS = 2
R_DEV = 8
CAP = 64
ROWS = 256
MOVE = 4
N_DP = 32


def aligned_parts(key):
    span = LAT + ROPE - LAT // 2
    keys = jax.random.split(key, 7)
    chosen = jax.random.randint(keys[0], (ROWS,), 0, 8) == 0
    chosen = chosen.at[0].set(True)
    power = jax.random.randint(keys[1], (ROWS,), 0, 3).astype(jnp.float32)
    strength = jnp.exp2(power).at[0].set(4.0)
    which = jax.random.randint(keys[2], (ROWS,), 0, STEPS)
    heads = jax.random.randint(keys[3], (ROWS, H), 0, 2) == 1
    heads = heads.at[:, 0].set(True)
    pattern = (2 * jax.random.randint(keys[4], (ROWS, span), 0, 2) - 1).astype(jnp.float32)
    magnitude = jax.random.uniform(keys[5], (ROWS, span), minval=4.0, maxval=6.0)
    target = jax.random.uniform(keys[6], (ROWS,), minval=1.3, maxval=2.7)
    spacing = target * math.sqrt(VD + ROPE) / (strength * span)
    return (chosen, strength, which, heads, pattern, magnitude, spacing)


def draw_cache(key, part):
    chosen, strength, which, heads, pattern, magnitude, spacing = aligned_parts(key)
    key = jax.random.fold_in(key, 5)
    extent = (ROWS, CAP, LAT + ROPE)
    background = jnp.clip(jax.random.normal(key, extent), -6.0, 6.0)
    half = LAT // 2
    marked = chosen[:, None]
    leading = jnp.where(marked, pattern * magnitude, background[:, 0, half:])
    trailing = jnp.where(marked, pattern * (magnitude - spacing[:, None]), background[:, 1, half:])
    background = background.at[:, 0, half:].set(leading)
    background = background.at[:, 1, half:].set(trailing)
    return background.astype(jnp.bfloat16)


def draw_queries(key, part):
    chosen, strength, which, heads, pattern, magnitude, spacing = aligned_parts(key)
    key = jax.random.fold_in(key, 7)
    extent = (ROWS, STEPS, H, LAT + ROPE)
    background = jnp.clip(0.5 * jax.random.normal(key, extent), -4.0, 4.0)
    half = LAT // 2
    span = LAT + ROPE - half
    tail = jnp.broadcast_to((strength[:, None] * pattern)[:, None, None, :], (ROWS, STEPS, H, span))
    aligned = jnp.concatenate([0.04 * background[..., :half], tail], axis=3)
    step_ids = jnp.arange(STEPS, dtype=jnp.int32)
    picked = chosen[:, None, None] & (step_ids[None, :, None] == which[:, None, None]) & heads[:, None, :]
    return jnp.where(picked[..., None], aligned, background).astype(jnp.bfloat16)


def draw_lengths(key, part):
    key = jax.random.fold_in(key, 11)
    peers = ROWS // R_DEV
    first, second = jax.random.split(key)
    heavy = jax.random.randint(first, (peers, 1), 0, 2)
    ceiling = jnp.where(heavy == 1, CAP - STEPS, max(CAP // 8, 3))
    raw = jax.random.randint(second, (peers, R_DEV), 0, CAP)
    values = (2 + raw % (ceiling - 1)).reshape(-1)
    values = values.at[0].set(CAP - STEPS)
    return values.astype(jnp.int32)


def draw_outgoing(key, part):
    key = jax.random.fold_in(key, 23)
    peers = ROWS // R_DEV
    keys = jax.random.split(key, peers)
    orders = jax.vmap(lambda single: jax.random.permutation(single, R_DEV))(keys)
    return orders[:, :MOVE].reshape(-1).astype(jnp.int32)


def draw_targets(key, part):
    key = jax.random.fold_in(key, 37)
    peers = ROWS // R_DEV
    first, second = jax.random.split(key)
    labels = jax.random.permutation(first, peers)
    inverse = jnp.argsort(labels)
    offsets = 1 + jax.random.permutation(second, peers - 1)[:MOVE]
    position = (inverse[:, None] + offsets[None, :]) % peers
    return labels[position].reshape(-1).astype(jnp.int32)


def levels(own_key, shape, cuts, smallest, top_value):
    def one(dim, shards_of):
        draws = jax.random.uniform(jax.random.fold_in(jax.random.fold_in(own_key, 6), dim), (shards_of,), jnp.float32, smallest / len(cuts), top_value / len(cuts))
        return jnp.repeat(jnp.exp(draws), shape[dim] // shards_of).reshape((-1,) + (1,) * (len(shape) - dim - 1))

    loudness = one(*cuts[0])
    for cut in cuts[1:]:
        loudness = loudness * one(*cut)
    return loudness


def bell_draw(own_key, shape, scale, reach, cuts=(), kind=jnp.bfloat16):
    loudness = levels(own_key, shape, cuts, -0.22, 0.18) if cuts else 1.0
    array = jax.random.normal(own_key, shape, jnp.float32) * scale * loudness
    return jnp.minimum(jnp.maximum(array, -reach), reach).astype(kind)


def setup_inputs(seed: int = 0, part: int = 0) -> dict:
    key_list = jax.random.split(jax.random.key(seed), 9)
    part_splits = jax.random.split(jax.random.fold_in(key_list[8], part), 9)
    return {
        "cache": draw_cache(jax.random.fold_in(jax.random.fold_in(key_list[8], part), 71), part),
        "lengths": draw_lengths(jax.random.fold_in(jax.random.fold_in(key_list[8], part), 71), part),
        "queries": draw_queries(jax.random.fold_in(jax.random.fold_in(key_list[8], part), 71), part),
        "fresh": bell_draw(part_splits[3], (ROWS, STEPS, LAT + ROPE), 1.0, 6.0, ((0, 32),)),
        "w_uv": bell_draw(key_list[4], (H, LAT, VD), LAT ** -0.5, 0.25, ((0, 32),)),
        "w_out": bell_draw(key_list[5], (H * VD, D), (H * VD) ** -0.5, 0.0625, ((0, 32),)),
        "outgoing": draw_outgoing(jax.random.fold_in(jax.random.fold_in(key_list[8], part), 71), part),
        "targets": draw_targets(jax.random.fold_in(jax.random.fold_in(key_list[8], part), 71), part),
    }


def reference(cache, lengths, queries, fresh, w_uv, w_out, outgoing, targets):
    peers = N_DP
    heads_dev = H // N_DP
    slots = jnp.arange(CAP, dtype=jnp.int32)
    updated = cache
    for step in range(STEPS):
        spot = (slots[None, :] == (lengths + step)[:, None])[:, :, None]
        updated = jnp.where(spot, fresh[:, step][:, None, :], updated)
    scale = 1.0 / math.sqrt(VD + ROPE)
    flat_q = queries.reshape(ROWS, STEPS * H, LAT + ROPE).astype(jnp.float32)
    scores = jnp.einsum('rqc,rkc->rqk', flat_q, updated.astype(jnp.float32)) * scale
    step_of = jnp.repeat(jnp.arange(STEPS, dtype=jnp.int32), H)
    limit = lengths[:, None] + step_of[None, :]
    allowed = slots[None, None, :] <= limit[:, :, None]
    scores = jnp.where(allowed, scores, -1e+30)
    top = lax.optimization_barrier(jnp.max(scores, axis=2, keepdims=True))
    weights = jnp.exp(scores - top)
    probs = (weights / lax.optimization_barrier(jnp.sum(weights, axis=2, keepdims=True))).astype(jnp.bfloat16)
    latent = jnp.einsum('rqk,rkl->rql', probs.astype(jnp.float32), updated[:, :, :LAT].astype(jnp.float32))
    latent = latent.astype(jnp.bfloat16).reshape(ROWS, STEPS, H, LAT)
    values = jnp.einsum('rshl,hlv->rshv', latent.astype(jnp.float32), w_uv.astype(jnp.float32)).astype(jnp.bfloat16)
    flat_v = values.reshape(ROWS * STEPS, peers, heads_dev * VD).transpose(1, 0, 2)
    groups = w_out.reshape(peers, heads_dev * VD, D)

    def add_group(total, pieces):
        part = jnp.dot(pieces[0], pieces[1], preferred_element_type=jnp.float32)
        part = lax.optimization_barrier(part.astype(jnp.bfloat16)).astype(jnp.float32)
        return (total + part, None)
    total, unused = lax.scan(add_group, jnp.zeros((ROWS * STEPS, D), jnp.float32), (flat_v, groups))
    attended = total.astype(jnp.bfloat16).reshape(ROWS, STEPS, D)
    moves = outgoing.reshape(peers, MOVE)
    dests = targets.reshape(peers, MOVE)
    local = jnp.arange(R_DEV, dtype=jnp.int32)
    base = (jnp.arange(peers, dtype=jnp.int32) * R_DEV)[:, None]
    moved = jnp.any(local[None, :, None] == moves[:, None, :], axis=2)
    keep_key = moved.astype(jnp.int32) * R_DEV + local[None, :]
    kept = jnp.argsort(keep_key, axis=1)[:, :R_DEV - MOVE].astype(jnp.int32) + base
    source_rows = (base + moves).reshape(-1)
    order_key = (dests * peers + jnp.arange(peers, dtype=jnp.int32)[:, None]).reshape(-1)
    received = source_rows[jnp.argsort(order_key)].reshape(peers, MOVE)
    new_order = jnp.concatenate([kept, received.astype(jnp.int32)], axis=1).reshape(-1)
    return (updated[new_order], attended[new_order])
```

```python
import math

import jax
import jax.numpy as jnp
from jax import lax
from jax.experimental import pallas as pl
from jax.experimental.pallas import tpu as pltpu
from jax.sharding import PartitionSpec as P

D = 7168
LAT = 512
ENT = 576
VD = 128
ROPE = 64
CAP = 64
ROWS = 8
MOVE = 4
SUBS = 7
SUB = D // SUBS
HALF = SUB // 2
MESH = pl.DeviceIdType.MESH
BF = jnp.bfloat16
F32 = jnp.float32
I32 = jnp.int32


def iota(shape, dim):
    return lax.broadcasted_iota(I32, shape, dim)


def one_hot(mask):
    return jnp.where(mask, 1.0, 0.0).astype(BF)


def mm(a, b):
    return jnp.dot(a, b, preferred_element_type=F32)


def kernel(
    len_s, out_s, tgt_s, fresh_v, cache_h, q_h, wuv_h, wout_h,
    nc_h, att_h,
    upd, q_v, wuv, wout, lat, in1, in2, vals, gall,
    part, rl, mg, ac, p2, rl2, mg2, ac2, att,
    cand, sib, sel, fin, swp, outc, tabv, tabs,
    lsem, gsem, grec, wsem, wrec, s1, r1, s2, r2, sv, rv,
    srs, rrs, cs, cr, osem,
):
    dp = lax.axis_index("dp")
    x, y, c = dp // 8, (dp // 2) % 4, dp % 2
    f = x + c * (y - x)
    g = y + c * (x - y)

    def dev(ff, gg, cc):
        xx = ff + c * (gg - ff)
        yy = gg + c * (ff - gg)
        return (xx * 4 + yy) * 2 + cc

    def on_f(k):
        return {"dp": dev((f + k) % 4, g, c)}

    def on_g(k):
        return {"dp": dev(f, (g + k) % 4, c)}

    sibling = {"dp": dev(f, g, 1 - c)}

    def send(src, dst, ss, rs, device):
        copy = pltpu.make_async_remote_copy(
            src_ref=src, dst_ref=dst, send_sem=ss, recv_sem=rs, device_id=device, device_id_type=MESH
        )
        copy.start()
        return copy

    loads = [
        pltpu.make_async_copy(cache_h, upd, lsem.at[0]),
        pltpu.make_async_copy(q_h, q_v, lsem.at[1]),
        pltpu.make_async_copy(wuv_h, wuv.at[pl.ds(2 * c, 2)], lsem.at[2]),
        pltpu.make_async_copy(wout_h, wout.at[pl.ds(pl.multiple_of(256 * c, 256), 256)], lsem.at[3]),
    ]
    for load in loads:
        load.start()

    barrier = pltpu.get_barrier_semaphore()
    for k in (1, 2, 3):
        pl.semaphore_signal(barrier, inc=1, device_id=on_f(k), device_id_type=MESH)
        pl.semaphore_signal(barrier, inc=1, device_id=on_g(k), device_id_type=MESH)
    pl.semaphore_signal(barrier, inc=1, device_id=sibling, device_id_type=MESH)

    lane = iota((1, 128), 1)
    slot_lane = (lane >> 1) & 7
    dest_row = jnp.full((1, 128), -1.0, F32)
    target_row = jnp.zeros((1, 128), F32)
    for m in range(MOVE):
        goal = tgt_s[m].astype(F32)
        dest_row = jnp.where(slot_lane == out_s[m], goal, dest_row)
        target_row = jnp.where((lane & 3) == m, goal, target_row)
    row_of = iota((8, 128), 0)
    gall[c, 0, 0] = jnp.where(row_of == 0, dest_row, target_row)

    pl.semaphore_wait(barrier, 7)

    g1 = [send(gall.at[c, 0, 0], gall.at[c, 0, k], gsem.at[k - 1], grec.at[k - 1], on_f(k)) for k in (1, 2, 3)]

    loads[0].wait()
    slot = iota((CAP, 1), 0)
    for r in range(ROWS):
        fresh = fresh_v[r].astype(F32)
        old = upd[r].astype(F32)
        new = jnp.where(slot == len_s[r], fresh[0:1], old)
        new = jnp.where(slot == len_s[r] + 1, fresh[1:2], new)
        upd[r] = new.astype(BF)
    mine = pl.multiple_of(c * 32, 32)
    theirs = pl.multiple_of((1 - c) * 32, 32)
    for m in range(MOVE):
        sib[m] = upd[out_s[m], pl.ds(theirs, 32)]
        cand[0, c, m] = upd[out_s[m], pl.ds(mine, 32)]
    c0 = send(sib, cand.at[0, c], cs.at[0], cr.at[0], sibling)
    w0 = send(wuv_h, wuv.at[pl.ds(2 * c, 2)], wsem.at[0], wrec.at[0], sibling)
    w1 = send(wout_h, wout.at[pl.ds(pl.multiple_of(256 * c, 256), 256)], wsem.at[1], wrec.at[1], sibling)

    ro = iota((512, 1), 0)
    of, og, oh, orow, ostep = ro >> 7, (ro >> 5) & 3, (ro >> 3) & 3, (ro >> 1) & 3, ro & 1
    ox = of + c * (og - of)
    oy = og + c * (of - og)
    wanted = orow * 128 + ostep * 64 + (ox * 4 + oy) * 4 + oh
    turn = one_hot(iota((512, 512), 1) == wanted)
    qi = iota((512, 256), 0)
    ki = iota((512, 256), 1)
    same_row = (qi >> 7) == (ki >> 6)
    ahead = (ki & 63) - ((qi >> 6) & 1)
    klane = iota((1, 256), 1) >> 6
    scale = 1.0 / math.sqrt(VD + ROPE)

    loads[1].wait()
    l1 = {}
    for grp in range(2):
        queries = q_v[4 * grp : 4 * grp + 4].reshape(512, ENT)
        keys = upd[4 * grp : 4 * grp + 4].reshape(256, ENT)
        scores = lax.dot_general(queries, keys, (((1,), (1,)), ((), ())), preferred_element_type=F32) * scale
        limit = jnp.zeros((1, 256), I32)
        for r in range(4):
            limit = jnp.where(klane == r, len_s[4 * grp + r], limit)
        scores = jnp.where(same_row & (ahead <= limit), scores, -1e30)
        weights = jnp.exp(scores - jnp.max(scores, axis=1, keepdims=True))
        probs = (weights / jnp.sum(weights, axis=1, keepdims=True)).astype(BF)
        turned = mm(turn, probs).astype(BF)
        latent = mm(turned, keys[:, :LAT]).astype(BF)
        lat[grp] = latent.reshape(4, 4, 32, LAT)
        for k in (1, 2, 3):
            l1[grp, k] = send(lat.at[grp, (f + k) % 4], in1.at[grp, k], s1.at[grp, k - 1], r1.at[grp, k - 1], on_f(k))

    for copy in g1:
        copy.wait_recv()
    g2 = [send(gall.at[c, 0], gall.at[c, k], gsem.at[2 + k], grec.at[2 + k], on_g(k)) for k in (1, 2, 3)]
    c0.wait_recv()
    c1 = [send(cand.at[0], cand.at[k], cs.at[k], cr.at[k], on_f(k)) for k in (1, 2, 3)]

    l2 = {}
    for grp in range(2):
        for k in range(4):
            if k:
                l1[grp, k].wait_recv()
                block = in1.at[grp, k]
            else:
                block = lat.at[grp, f]
            for j in (1, 2, 3):
                l2[grp, k, j] = send(
                    block.at[(g + j) % 4], in2.at[j, k, grp], s2.at[grp, k, j - 1], r2.at[grp, k, j - 1], on_g(j)
                )
            if k:
                in2[0, k, grp] = in1[grp, k, g]
            else:
                in2[0, k, grp] = lat[grp, f, g]

    for copy in g2:
        copy.wait_recv()
    g3 = send(gall.at[c], gall.at[c], gsem.at[6], grec.at[6], sibling)

    def source(l):
        cs_, dg_, df_ = l >> 8, (l >> 6) & 3, (l >> 4) & 3
        fs = (x + cs_ * (y - x) - df_) & 3
        gs = (y + cs_ * (x - y) - dg_) & 3
        return ((fs + cs_ * (gs - fs)) * 4 + gs + cs_ * (fs - gs)) * 2 + cs_

    wide = iota((1, 512), 1)
    tall = iota((512, 1), 0)
    from_w, from_t = source(wide), source(tall)
    slot_w, slot_t = (wide >> 1) & 7, (tall >> 1) & 7
    even = (tall & 1) == 0
    before = one_hot(even & (from_t < from_w))
    within = one_hot(even & (from_t == from_w) & (slot_t < slot_w))
    nr = iota((256, 1), 0)
    nf, ng = nr >> 6, (nr >> 4) & 3
    ndev = ((nf + c * (ng - nf)) * 4 + ng + c * (nf - ng)) * 2 + c
    nslot, nstep = (nr >> 1) & 7, nr & 1

    g3.wait_recv()
    rows = gall[...].reshape(32, 8, 128)
    sub8 = iota((8, 128), 0)
    lane8 = iota((8, 128), 1) >> 4
    pieces = []
    for v in range(4):
        total = jnp.zeros((1, 128), F32)
        for b in range(8):
            total = total + jnp.where((lane >> 4) == b, rows[8 * v + b][0:1], 0.0)
        pieces.append(total)
    dest_w = jnp.concatenate(pieces, axis=1).astype(I32)
    comes = dest_w == ndev
    stays = (dest_w < 0) & (from_w == ndev)
    rank_in = mm(one_hot(comes), before)
    rank_stay = mm(one_hot(stays), within)
    place = jnp.where(comes, rank_in + 4.0, jnp.where(stays, rank_stay, -1.0))
    order = one_hot((place == nslot.astype(F32)) & ((wide & 1) == nstep))

    table = jnp.zeros((1, 128), F32)
    l_dg, l_df, l_sc = lane >> 5, (lane >> 3) & 3, (lane >> 2) & 1
    for sc in range(2):
        for a in range(4):
            for b in range(4):
                row = rows[sc * 16 + a * 4 + b][1:2]
                swapped = sc + c - 2 * sc * c
                la = a + swapped * (b - a)
                lb = b + swapped * (a - b)
                table = table + jnp.where((l_sc == sc) & (l_dg == la) & (l_df == lb), row, 0.0)
    table = table.astype(I32)
    lt, lw = iota((128, 128), 0), iota((128, 128), 1)
    earlier = one_hot(((lt >> 5) == (lw >> 5)) & (lt < lw))

    def mover(l):
        fs = (f - ((l >> 3) & 3)) & 3
        gs = (g - (l >> 5)) & 3
        return ((fs + c * (gs - fs)) * 4 + gs + c * (fs - gs)) * 2 + ((l >> 2) & 1)

    lower = one_hot(mover(iota((128, 1), 0)) < mover(lane))
    tr = iota((32, 128), 0)
    tdg, tcore, tk = tr >> 3, (tr >> 2) & 1, tr & 3
    tl = iota((32, 128), 1)
    tg = (g + tdg) & 3
    tdev = ((f + c * (tg - f)) * 4 + tg + c * (f - tg)) * 2 + tcore
    hit = (table == tdev) & (tl < 32)
    nth = mm(one_hot(hit), earlier)
    pick = jnp.sum(jnp.where(hit & (nth == tk.astype(F32)), tl, 0), axis=1, keepdims=True)
    ur = iota((8, 128), 0)
    ucore, uj = ur >> 2, ur & 3
    udev = ((f + c * (g - f)) * 4 + g + c * (f - g)) * 2 + ucore
    own = table == udev
    spot = (lane >> 5) * 8 + ucore * 4 + mm(one_hot(own), earlier).astype(I32)
    turn_in = mm(one_hot(own), lower)
    last = jnp.sum(jnp.where(own & (turn_in == uj.astype(F32)), spot, 0), axis=1, keepdims=True)
    tabv[0:32] = jnp.broadcast_to(pick, (32, 128))
    tabv[32:40] = jnp.broadcast_to(last, (8, 128))
    tcopy = pltpu.make_async_copy(tabv, tabs, lsem.at[4])
    tcopy.start()
    tcopy.wait()

    for copy in c1:
        copy.wait_recv()
    c2 = []
    for j in (1, 2, 3, 0):
        for i in range(8):
            which = tabs[j * 8 + i, 0]
            chosen = cand[which >> 3, (which >> 2) & 1, which & 3]
            if j:
                sel[j - 1, i] = chosen
            else:
                fin[0, i] = chosen
        if j:
            c2.append(send(sel.at[j - 1], fin.at[j], cs.at[3 + j], cr.at[3 + j], on_g(j)))

    loads[2].wait()
    w0.wait_recv()
    swaps = []
    for j in range(4):
        if j:
            for grp in range(2):
                for k in range(4):
                    l2[grp, k, j].wait_recv()
        block = in2[j].reshape(256, LAT)
        for h in range(4):
            value = mm(block, wuv[h]).reshape(8, 4, 8, VD)[:, h].reshape(64, VD)
            vals[c, pl.ds(64 * j, 64), pl.ds(VD * h, VD)] = value.astype(BF)
        swaps.append(
            send(vals.at[c, pl.ds(64 * j, 64)], vals.at[c, pl.ds(64 * j, 64)], sv.at[j], rv.at[j], sibling)
        )
    for copy in swaps:
        copy.wait_recv()
    flat = mm(order, vals[...].reshape(512, 512)).astype(BF)
    loads[3].wait()
    w1.wait_recv()

    f1, f2, f3 = (f + 1) % 4, (f + 2) % 4, (f + 3) % 4
    h1, h2, h3 = (g + 1) % 4, (g + 2) % 4, (g + 3) % 4
    low, high = pl.ds(0, 32), pl.ds(32, 32)
    left, right = pl.ds(0, HALF), pl.ds(HALF, HALF)

    def rs(s, i, src, dst, device):
        return pltpu.make_async_remote_copy(
            src_ref=src, dst_ref=dst, send_sem=srs.at[s, i], recv_sem=rrs.at[s, i],
            device_id=device, device_id_type=MESH,
        )

    def copy_of(s, i):
        table = (
            lambda: rs(s, 0, part.at[s, f2, low], rl.at[s, 0], on_f(1)),
            lambda: rs(s, 1, part.at[s, f2, high], rl.at[s, 1], on_f(3)),
            lambda: rs(s, 2, part.at[s, f1, high], ac.at[s, 0, high], on_f(1)),
            lambda: rs(s, 3, part.at[s, f3, low], ac.at[s, 1, low], on_f(3)),
            lambda: rs(s, 4, mg.at[s, 0], ac.at[s, 0, low], on_f(1)),
            lambda: rs(s, 5, mg.at[s, 1], ac.at[s, 1, high], on_f(3)),
            lambda: rs(s, 6, p2.at[s, h2, :, left], rl2.at[s, 0], on_g(1)),
            lambda: rs(s, 7, p2.at[s, h2, :, right], rl2.at[s, 1], on_g(3)),
            lambda: rs(s, 8, p2.at[s, h1, :, right], ac2.at[s, 0, :, right], on_g(1)),
            lambda: rs(s, 9, p2.at[s, h3, :, left], ac2.at[s, 1, :, left], on_g(3)),
            lambda: rs(s, 10, mg2.at[s, 0], ac2.at[s, 0, :, left], on_g(1)),
            lambda: rs(s, 11, mg2.at[s, 1], ac2.at[s, 1, :, right], on_g(3)),
        )
        return table[i]()

    def step(t, carry):
        @pl.when(t < SUBS)
        def _():
            s = t
            cols = pl.ds(pl.multiple_of(s * SUB, SUB), SUB)
            part[s] = mm(flat, wout[:, cols]).astype(BF).reshape(4, 64, SUB)
            for i in range(4):
                copy_of(s, i).start()

        @pl.when((t >= 1) & (t < SUBS + 1))
        def _():
            s = t - 1
            copy_of(s, 0).wait_recv()
            mg[s, 0] = (part[s, f1, low].astype(F32) + rl[s, 0].astype(F32)).astype(BF)
            copy_of(s, 4).start()
            copy_of(s, 1).wait_recv()
            mg[s, 1] = (part[s, f3, high].astype(F32) + rl[s, 1].astype(F32)).astype(BF)
            copy_of(s, 5).start()

        @pl.when((t >= 2) & (t < SUBS + 2))
        def _():
            s = t - 2
            for i in (2, 3, 4, 5):
                copy_of(s, i).wait_recv()
            whole = part[s, f].astype(F32) + ac[s, 0].astype(F32) + ac[s, 1].astype(F32)
            p2[s] = whole.astype(BF).reshape(4, 16, SUB)
            for i in (6, 7, 8, 9):
                copy_of(s, i).start()

        @pl.when((t >= 3) & (t < SUBS + 3))
        def _():
            s = t - 3
            copy_of(s, 6).wait_recv()
            mg2[s, 0] = (p2[s, h1, :, left].astype(F32) + rl2[s, 0].astype(F32)).astype(BF)
            copy_of(s, 10).start()
            copy_of(s, 7).wait_recv()
            mg2[s, 1] = (p2[s, h3, :, right].astype(F32) + rl2[s, 1].astype(F32)).astype(BF)
            copy_of(s, 11).start()

        @pl.when(t >= 4)
        def _():
            s = t - 4
            for i in (8, 9, 10, 11):
                copy_of(s, i).wait_recv()
            whole = p2[s, g].astype(F32) + ac2[s, 0].astype(F32) + ac2[s, 1].astype(F32)
            att[s] = whole.astype(BF)
            cols = pl.ds(pl.multiple_of(s * SUB, SUB), SUB)
            pltpu.make_async_copy(att.at[s], att_h.at[:, cols], osem.at[s]).start()

        return carry

    lax.fori_loop(0, SUBS + 4, step, 0)

    for copy in c2:
        copy.wait_recv()
    for j in range(MOVE):
        there = tabs[32 + (1 - c) * 4 + j, 0]
        here = tabs[32 + c * 4 + j, 0]
        swp[j] = fin[there >> 3, there & 7]
        outc[MOVE + j, pl.ds(mine, 32)] = fin[here >> 3, here & 7]
    c3 = send(swp, outc.at[pl.ds(MOVE, MOVE), pl.ds(mine, 32)], cs.at[7], cr.at[7], sibling)
    kept = [0] * MOVE
    count = 0
    for r in range(ROWS):
        gone = (out_s[0] == r) | (out_s[1] == r) | (out_s[2] == r) | (out_s[3] == r)
        stay = 1 - gone.astype(I32)
        for j in range(MOVE):
            kept[j] = kept[j] + jnp.where(count == j, stay * r, 0)
        count = count + stay
    for j in range(MOVE):
        outc[j] = upd[kept[j]]
    c3.wait_recv()
    finish = pltpu.make_async_copy(outc, nc_h, lsem.at[5])
    finish.start()

    for copy in g1 + g2 + [g3, c0, w0, w1] + c1 + c2 + swaps + [c3]:
        copy.wait_send()
    for copy in list(l1.values()) + list(l2.values()):
        copy.wait_send()

    def drain(s, carry):
        for i in range(12):
            copy_of(s, i).wait_send()
        cols = pl.ds(pl.multiple_of(s * SUB, SUB), SUB)
        pltpu.make_async_copy(att.at[s], att_h.at[:, cols], osem.at[s]).wait()
        return carry

    lax.fori_loop(0, SUBS, drain, 0)
    finish.wait()


def per_device(cache, lengths, queries, fresh, w_uv, w_out, outgoing, targets):
    smem = pl.BlockSpec(memory_space=pltpu.SMEM)
    hbm = pl.BlockSpec(memory_space=pl.ANY)
    dma = pltpu.SemaphoreType.DMA
    scratch = [
        pltpu.VMEM((ROWS, CAP, ENT), BF),
        pltpu.VMEM((ROWS, 128, ENT), BF),
        pltpu.VMEM((4, LAT, VD), BF),
        pltpu.VMEM((512, D), BF),
        pltpu.VMEM((2, 4, 4, 32, LAT), BF),
        pltpu.VMEM((2, 4, 4, 32, LAT), BF),
        pltpu.VMEM((4, 4, 2, 32, LAT), BF),
        pltpu.VMEM((2, 256, 512), BF),
        pltpu.VMEM((2, 4, 4, 8, 128), F32),
        pltpu.VMEM((SUBS, 4, 64, SUB), BF),
        pltpu.VMEM((SUBS, 2, 32, SUB), BF),
        pltpu.VMEM((SUBS, 2, 32, SUB), BF),
        pltpu.VMEM((SUBS, 2, 64, SUB), BF),
        pltpu.VMEM((SUBS, 4, 16, SUB), BF),
        pltpu.VMEM((SUBS, 2, 16, HALF), BF),
        pltpu.VMEM((SUBS, 2, 16, HALF), BF),
        pltpu.VMEM((SUBS, 2, 16, SUB), BF),
        pltpu.VMEM((SUBS, 16, SUB), BF),
        pltpu.VMEM((4, 2, MOVE, 32, ENT), BF),
        pltpu.VMEM((MOVE, 32, ENT), BF),
        pltpu.VMEM((3, 8, 32, ENT), BF),
        pltpu.VMEM((4, 8, 32, ENT), BF),
        pltpu.VMEM((MOVE, 32, ENT), BF),
        pltpu.VMEM((ROWS, CAP, ENT), BF),
        pltpu.VMEM((40, 128), I32),
        pltpu.SMEM((40, 128), I32),
        dma((6,)),
        dma((7,)), dma((7,)),
        dma((2,)), dma((2,)),
        dma((2, 3)), dma((2, 3)),
        dma((2, 4, 3)), dma((2, 4, 3)),
        dma((4,)), dma((4,)),
        dma((SUBS, 12)), dma((SUBS, 12)),
        dma((8,)), dma((8,)),
        dma((SUBS,)),
    ]
    new_cache, attended = pl.pallas_call(
        kernel,
        out_shape=(
            jax.ShapeDtypeStruct((ROWS, CAP, ENT), BF),
            jax.ShapeDtypeStruct((2 * ROWS, D), BF),
        ),
        in_specs=[smem, smem, smem, pl.BlockSpec(memory_space=pltpu.VMEM), hbm, hbm, hbm, hbm],
        out_specs=(hbm, hbm),
        scratch_shapes=scratch,
        compiler_params=pltpu.CompilerParams(
            collective_id=0, has_side_effects=True, vmem_limit_bytes=48 * 1024 * 1024
        ),
        cost_estimate=pl.CostEstimate(flops=4 * 10**9, bytes_accessed=8 * 10**6, transcendentals=10**6),
        name="mla_decode",
    )(lengths, outgoing, targets, fresh, cache, queries.reshape(ROWS, 128, ENT), w_uv, w_out)
    return new_cache, attended.reshape(ROWS, 2, D)


def solution(mesh):
    in_specs = (
        P(("rep", "dp"), None, None),
        P(("rep", "dp")),
        P(("rep", "dp"), None, None, None),
        P(("rep", "dp"), None, None),
        P("dp", None, None),
        P("dp", None),
        P(("rep", "dp")),
        P(("rep", "dp")),
    )
    out_specs = (P(("rep", "dp"), None, None), P(("rep", "dp"), None, None))
    return jax.shard_map(
        per_device, mesh=mesh, in_specs=in_specs, out_specs=out_specs, check_vma=False
    )
```

```python
import math

import jax
import jax.numpy as jnp
from jax import lax
from jax.experimental import pallas as pl
from jax.experimental.pallas import tpu as pltpu
from jax.sharding import PartitionSpec as P

D = 7168
LAT = 512
ENT = 576
VD = 128
ROPE = 64
CAP = 64
ROWS = 8
MOVE = 4
SUBS = 7
SUB = D // SUBS
HALF = SUB // 2
MESH = pl.DeviceIdType.MESH
BF = jnp.bfloat16
F32 = jnp.float32
I32 = jnp.int32


def iota(shape, dim):
    return lax.broadcasted_iota(I32, shape, dim)


def one_hot(mask):
    return jnp.where(mask, 1.0, 0.0).astype(BF)


def mm(a, b):
    return jnp.dot(a, b, preferred_element_type=F32)


def kernel(
    len_h, out_h, tgt_h, fresh_h, cache_h, q_h, wuv_h, wout_h,
    nc_v, att_v,
    len_s, out_s, tgt_s, fresh_v,
    turn, before, within, earlier, lower, order, flat,
    upd, q_v, wuv, wout, lat, in1, in2, vals, gall,
    part, rl, mg, ac, p2, rl2, mg2, ac2,
    cand, sib, sel, fin, swp, swr, tabv, tabs,
    lsem, gsem, grec, wsem, wrec, s1, r1, s2, r2, sv, rv,
    srs, rrs, cs, cr, cks, ckr,
):
    dp = lax.axis_index("dp")
    x, y, c = dp // 8, (dp // 2) % 4, dp % 2
    f = x + c * (y - x)
    g = y + c * (x - y)

    def dev(ff, gg, cc):
        xx = ff + c * (gg - ff)
        yy = gg + c * (ff - gg)
        return (xx * 4 + yy) * 2 + cc

    def on_f(k):
        return {"dp": dev((f + k) % 4, g, c)}

    def on_g(k):
        return {"dp": dev(f, (g + k) % 4, c)}

    sibling = {"dp": dev(f, g, 1 - c)}

    def send(src, dst, ss, rs, device):
        copy = pltpu.make_async_remote_copy(
            src_ref=src, dst_ref=dst, send_sem=ss, recv_sem=rs, device_id=device, device_id_type=MESH
        )
        copy.start()
        return copy

    small = [
        pltpu.make_async_copy(out_h, out_s, lsem.at[6]),
        pltpu.make_async_copy(tgt_h, tgt_s, lsem.at[7]),
        pltpu.make_async_copy(len_h, len_s, lsem.at[8]),
        pltpu.make_async_copy(fresh_h, fresh_v, lsem.at[9]),
    ]
    loads = [
        pltpu.make_async_copy(cache_h, upd, lsem.at[0]),
        pltpu.make_async_copy(q_h, q_v, lsem.at[1]),
        pltpu.make_async_copy(wuv_h, wuv.at[pl.ds(2 * c, 2)], lsem.at[2]),
        pltpu.make_async_copy(wout_h, wout.at[pl.ds(pl.multiple_of(256 * c, 256), 256)], lsem.at[3]),
    ]
    for load in small + loads:
        load.start()

    barrier = pltpu.get_barrier_semaphore()
    for k in (1, 2, 3):
        pl.semaphore_signal(barrier, inc=1, device_id=on_f(k), device_id_type=MESH)
        pl.semaphore_signal(barrier, inc=1, device_id=on_g(k), device_id_type=MESH)
    pl.semaphore_signal(barrier, inc=1, device_id=sibling, device_id_type=MESH)

    ro = iota((512, 1), 0)
    of, og, oh, orow, ostep = ro >> 7, (ro >> 5) & 3, (ro >> 3) & 3, (ro >> 1) & 3, ro & 1
    ox = of + c * (og - of)
    oy = og + c * (of - og)
    wanted = orow * 128 + ostep * 64 + (ox * 4 + oy) * 4 + oh
    turn[...] = one_hot(iota((512, 512), 1) == wanted)

    def source(l):
        cs_, dg_, df_ = l >> 8, (l >> 6) & 3, (l >> 4) & 3
        fs = (x + cs_ * (y - x) - df_) & 3
        gs = (y + cs_ * (x - y) - dg_) & 3
        return ((fs + cs_ * (gs - fs)) * 4 + gs + cs_ * (fs - gs)) * 2 + cs_

    wide = iota((1, 512), 1)
    tall = iota((512, 1), 0)
    from_w, from_t = source(wide), source(tall)
    slot_w, slot_t = (wide >> 1) & 7, (tall >> 1) & 7
    even = (tall & 1) == 0
    before[...] = one_hot(even & (from_t < from_w))
    within[...] = one_hot(even & (from_t == from_w) & (slot_t < slot_w))
    lt, lw = iota((128, 128), 0), iota((128, 128), 1)
    lane = iota((1, 128), 1)

    def mover(l):
        fs = (f - ((l >> 3) & 3)) & 3
        gs = (g - (l >> 5)) & 3
        return ((fs + c * (gs - fs)) * 4 + gs + c * (fs - gs)) * 2 + ((l >> 2) & 1)

    earlier[...] = one_hot(((lt >> 5) == (lw >> 5)) & (lt < lw))
    lower[...] = one_hot(mover(iota((128, 1), 0)) < mover(lane))

    small[0].wait()
    small[1].wait()
    slot_lane = (lane >> 1) & 7
    dest_row = jnp.full((1, 128), -1.0, F32)
    target_row = jnp.zeros((1, 128), F32)
    for m in range(MOVE):
        goal = tgt_s[m].astype(F32)
        dest_row = jnp.where(slot_lane == out_s[m], goal, dest_row)
        target_row = jnp.where((lane & 3) == m, goal, target_row)
    row_of = iota((8, 128), 0)
    gall[c, 0, 0] = jnp.where(row_of == 0, dest_row, target_row)

    loads[0].wait()
    small[2].wait()
    small[3].wait()
    slot = iota((CAP, 1), 0)
    for r in range(ROWS):
        fresh = fresh_v[r].astype(F32)
        old = upd[r].astype(F32)
        new = jnp.where(slot == len_s[r], fresh[0:1], old)
        new = jnp.where(slot == len_s[r] + 1, fresh[1:2], new)
        upd[r] = new.astype(BF)
    mine = pl.multiple_of(c * 32, 32)
    theirs = pl.multiple_of((1 - c) * 32, 32)
    for m in range(MOVE):
        sib[m] = upd[out_s[m], pl.ds(theirs, 32)]
        cand[0, c, m] = upd[out_s[m], pl.ds(mine, 32)]

    pl.semaphore_wait(barrier, 7)
    g1 = [send(gall.at[c, 0, 0], gall.at[c, 0, k], gsem.at[k - 1], grec.at[k - 1], on_f(k)) for k in (1, 2, 3)]
    c0 = send(sib, cand.at[0, c], cs.at[0], cr.at[0], sibling)

    def pass_rows(k, sc, src):
        return send(src, cand.at[k, sc], cks.at[k - 1, sc], ckr.at[k - 1, sc], on_f(k if k != 2 else 1 + 2 * sc))

    c1 = [pass_rows(k, c, cand.at[0, c]) for k in (1, 3)]
    w0 = send(wuv_h, wuv.at[pl.ds(2 * c, 2)], wsem.at[0], wrec.at[0], sibling)
    w1 = send(wout_h, wout.at[pl.ds(pl.multiple_of(256 * c, 256), 256)], wsem.at[1], wrec.at[1], sibling)

    qi = iota((512, 256), 0)
    ki = iota((512, 256), 1)
    same_row = (qi >> 7) == (ki >> 6)
    ahead = (ki & 63) - ((qi >> 6) & 1)
    klane = iota((1, 256), 1) >> 6
    scale = 1.0 / math.sqrt(VD + ROPE)

    loads[1].wait()
    l1 = {}
    l2 = {}

    def onward(grp, k, block):
        for j in (1, 3, 2):
            l2[grp, k, j] = send(
                block.at[(g + j) % 4], in2.at[j, k, grp], s2.at[grp, k, j - 1], r2.at[grp, k, j - 1], on_g(j)
            )

    for grp in range(2):
        queries = q_v[4 * grp : 4 * grp + 4].reshape(512, ENT)
        keys = upd[4 * grp : 4 * grp + 4].reshape(256, ENT)
        scores = lax.dot_general(queries, keys, (((1,), (1,)), ((), ())), preferred_element_type=F32) * scale
        limit = jnp.zeros((1, 256), I32)
        for r in range(4):
            limit = jnp.where(klane == r, len_s[4 * grp + r], limit)
        scores = jnp.where(same_row & (ahead <= limit), scores, -1e30)
        weights = jnp.exp(scores - jnp.max(scores, axis=1, keepdims=True))
        probs = (weights / jnp.sum(weights, axis=1, keepdims=True)).astype(BF)
        turned = mm(turn[...], probs).astype(BF)
        latent = mm(turned, keys[:, :LAT]).astype(BF)
        lat[grp] = latent.reshape(4, 4, 32, LAT)
        for k in (2, 1, 3):
            l1[grp, k] = send(lat.at[grp, (f + k) % 4], in1.at[grp, k], s1.at[grp, k - 1], r1.at[grp, k - 1], on_f(k))
        onward(grp, 0, lat.at[grp, f])
        in2[0, 0, grp] = lat[grp, f, g]

    c0.wait_recv()
    c1 += [pass_rows(k, 1 - c, cand.at[0, 1 - c]) for k in (1, 3)]
    for copy in g1:
        copy.wait_recv()
    g2 = [send(gall.at[c, 0], gall.at[c, k], gsem.at[2 + k], grec.at[2 + k], on_g(k)) for k in (1, 2, 3)]

    for grp in range(2):
        for k in (1, 3, 2):
            l1[grp, k].wait_recv()
            onward(grp, k, in1.at[grp, k])
            in2[0, k, grp] = in1[grp, k, g]

    for copy in g2:
        copy.wait_recv()
    g3 = send(gall.at[c], gall.at[c], gsem.at[6], grec.at[6], sibling)

    def arrived(k, sc):
        return pltpu.make_async_remote_copy(
            src_ref=cand.at[0, 0], dst_ref=cand.at[k, sc], send_sem=cks.at[k - 1, sc], recv_sem=ckr.at[k - 1, sc],
            device_id=on_f(k if k != 2 else 1 + 2 * sc), device_id_type=MESH,
        )

    arrived(1, 0).wait_recv()
    c1.append(pass_rows(2, 0, cand.at[1, 0]))
    arrived(3, 1).wait_recv()
    c1.append(pass_rows(2, 1, cand.at[3, 1]))

    nr = iota((256, 1), 0)
    nf, ng = nr >> 6, (nr >> 4) & 3
    ndev = ((nf + c * (ng - nf)) * 4 + ng + c * (nf - ng)) * 2 + c
    nslot, nstep = (nr >> 1) & 7, nr & 1

    g3.wait_recv()
    rows = gall[...].reshape(32, 8, 128)
    pieces = []
    for v in range(4):
        total = jnp.zeros((1, 128), F32)
        for b in range(8):
            total = total + jnp.where((lane >> 4) == b, rows[8 * v + b][0:1], 0.0)
        pieces.append(total)
    dest_w = jnp.concatenate(pieces, axis=1).astype(I32)
    comes = dest_w == ndev
    stays = (dest_w < 0) & (from_w == ndev)
    rank_in = mm(one_hot(comes), before[...])
    rank_stay = mm(one_hot(stays), within[...])
    place = jnp.where(comes, rank_in + 4.0, jnp.where(stays, rank_stay, -1.0))
    order[...] = one_hot((place == nslot.astype(F32)) & ((wide & 1) == nstep))

    table = jnp.zeros((1, 128), F32)
    l_dg, l_df, l_sc = lane >> 5, (lane >> 3) & 3, (lane >> 2) & 1
    for sc in range(2):
        for a in range(4):
            for b in range(4):
                row = rows[sc * 16 + a * 4 + b][1:2]
                swapped = sc + c - 2 * sc * c
                la = a + swapped * (b - a)
                lb = b + swapped * (a - b)
                table = table + jnp.where((l_sc == sc) & (l_dg == la) & (l_df == lb), row, 0.0)
    table = table.astype(I32)
    tr = iota((32, 128), 0)
    tdg, tcore, tk = tr >> 3, (tr >> 2) & 1, tr & 3
    tl = iota((32, 128), 1)
    tg = (g + tdg) & 3
    tdev = ((f + c * (tg - f)) * 4 + tg + c * (f - tg)) * 2 + tcore
    hit = (table == tdev) & (tl < 32)
    nth = mm(one_hot(hit), earlier[...])
    pick = jnp.sum(jnp.where(hit & (nth == tk.astype(F32)), tl, 0), axis=1, keepdims=True)
    ur = iota((8, 128), 0)
    ucore, uj = ur >> 2, ur & 3
    udev = ((f + c * (g - f)) * 4 + g + c * (f - g)) * 2 + ucore
    own = table == udev
    spot = (lane >> 5) * 8 + ucore * 4 + mm(one_hot(own), earlier[...]).astype(I32)
    turn_in = mm(one_hot(own), lower[...])
    last = jnp.sum(jnp.where(own & (turn_in == uj.astype(F32)), spot, 0), axis=1, keepdims=True)
    tabv[0:32] = jnp.broadcast_to(pick, (32, 128))
    tabv[32:40] = jnp.broadcast_to(last, (8, 128))
    tcopy = pltpu.make_async_copy(tabv, tabs, lsem.at[4])
    tcopy.start()

    loads[2].wait()
    w0.wait_recv()
    swaps = []
    for j in (0, 1, 3, 2):
        if j:
            for grp in range(2):
                for k in range(4):
                    l2[grp, k, j].wait_recv()
        block = in2[j].reshape(256, LAT)
        for h in range(4):
            value = mm(block, wuv[h]).reshape(8, 4, 8, VD)[:, h].reshape(64, VD)
            vals[c, pl.ds(64 * j, 64), pl.ds(VD * h, VD)] = value.astype(BF)
        swaps.append(
            send(vals.at[c, pl.ds(64 * j, 64)], vals.at[c, pl.ds(64 * j, 64)], sv.at[j], rv.at[j], sibling)
        )

    tcopy.wait()
    for k, sc in ((1, 1), (3, 0), (2, 0), (2, 1)):
        arrived(k, sc).wait_recv()
    c2 = []
    for j in (1, 3, 2, 0):
        for i in range(8):
            which = tabs[j * 8 + i, 0]
            chosen = cand[which >> 3, (which >> 2) & 1, which & 3]
            if j:
                sel[j - 1, i] = chosen
            else:
                fin[0, i] = chosen
        if j:
            c2.append(send(sel.at[j - 1], fin.at[j], cs.at[3 + j], cr.at[3 + j], on_g(j)))

    for copy in swaps:
        copy.wait_recv()
    flat[...] = mm(order[...], vals[...].reshape(512, 512)).astype(BF)
    loads[3].wait()
    w1.wait_recv()

    f1, f2, f3 = (f + 1) % 4, (f + 2) % 4, (f + 3) % 4
    h1, h2, h3 = (g + 1) % 4, (g + 2) % 4, (g + 3) % 4
    low, high = pl.ds(0, 32), pl.ds(32, 32)
    left, right = pl.ds(0, HALF), pl.ds(HALF, HALF)

    def rs(s, i, src, dst, device):
        return pltpu.make_async_remote_copy(
            src_ref=src, dst_ref=dst, send_sem=srs.at[s, i], recv_sem=rrs.at[s, i],
            device_id=device, device_id_type=MESH,
        )

    def copy_of(s, i):
        table = (
            lambda: rs(s, 0, part.at[s, f2, low], rl.at[s, 0], on_f(1)),
            lambda: rs(s, 1, part.at[s, f2, high], rl.at[s, 1], on_f(3)),
            lambda: rs(s, 2, part.at[s, f1, high], ac.at[s, 0, high], on_f(1)),
            lambda: rs(s, 3, part.at[s, f3, low], ac.at[s, 1, low], on_f(3)),
            lambda: rs(s, 4, mg.at[s, 0], ac.at[s, 0, low], on_f(1)),
            lambda: rs(s, 5, mg.at[s, 1], ac.at[s, 1, high], on_f(3)),
            lambda: rs(s, 6, p2.at[s, h2, :, left], rl2.at[s, 0], on_g(1)),
            lambda: rs(s, 7, p2.at[s, h2, :, right], rl2.at[s, 1], on_g(3)),
            lambda: rs(s, 8, p2.at[s, h1, :, right], ac2.at[s, 0, :, right], on_g(1)),
            lambda: rs(s, 9, p2.at[s, h3, :, left], ac2.at[s, 1, :, left], on_g(3)),
            lambda: rs(s, 10, mg2.at[s, 0], ac2.at[s, 0, :, left], on_g(1)),
            lambda: rs(s, 11, mg2.at[s, 1], ac2.at[s, 1, :, right], on_g(3)),
        )
        return table[i]()

    c3 = pltpu.make_async_remote_copy(
        src_ref=swp, dst_ref=swr, send_sem=cs.at[7], recv_sem=cr.at[7],
        device_id=sibling, device_id_type=MESH,
    )
    kept = [0] * MOVE
    count = 0
    for r in range(ROWS):
        gone = (out_s[0] == r) | (out_s[1] == r) | (out_s[2] == r) | (out_s[3] == r)
        stay = 1 - gone.astype(I32)
        for j in range(MOVE):
            kept[j] = kept[j] + jnp.where(count == j, stay * r, 0)
        count = count + stay

    def place_rows():
        for copy in c2:
            copy.wait_recv()
        for j in range(MOVE):
            there = tabs[32 + (1 - c) * 4 + j, 0]
            here = tabs[32 + c * 4 + j, 0]
            swp[j] = fin[there >> 3, there & 7]
            nc_v[MOVE + j, pl.ds(mine, 32)] = fin[here >> 3, here & 7]
        c3.start()
        for j in range(MOVE):
            nc_v[j] = upd[kept[j]]

    def store_rows():
        c3.wait_recv()
        for j in range(MOVE):
            nc_v[MOVE + j, pl.ds(theirs, 32)] = swr[j]

    def step(t, carry):
        pl.when(t == SUBS - 1)(place_rows)
        pl.when(t == SUBS + 1)(store_rows)

        @pl.when(t < SUBS)
        def _():
            s = t
            cols = pl.ds(pl.multiple_of(s * SUB, SUB), SUB)
            part[s] = mm(flat[...], wout[:, cols]).astype(BF).reshape(4, 64, SUB)
            for i in range(4):
                copy_of(s, i).start()

        @pl.when((t >= 1) & (t < SUBS + 1))
        def _():
            s = t - 1
            copy_of(s, 0).wait_recv()
            mg[s, 0] = (part[s, f1, low].astype(F32) + rl[s, 0].astype(F32)).astype(BF)
            copy_of(s, 4).start()
            copy_of(s, 1).wait_recv()
            mg[s, 1] = (part[s, f3, high].astype(F32) + rl[s, 1].astype(F32)).astype(BF)
            copy_of(s, 5).start()

        @pl.when((t >= 2) & (t < SUBS + 2))
        def _():
            s = t - 2
            for i in (2, 3, 4, 5):
                copy_of(s, i).wait_recv()
            whole = part[s, f].astype(F32) + ac[s, 0].astype(F32) + ac[s, 1].astype(F32)
            p2[s] = whole.astype(BF).reshape(4, 16, SUB)
            for i in (6, 7, 8, 9):
                copy_of(s, i).start()

        @pl.when((t >= 3) & (t < SUBS + 3))
        def _():
            s = t - 3
            copy_of(s, 6).wait_recv()
            mg2[s, 0] = (p2[s, h1, :, left].astype(F32) + rl2[s, 0].astype(F32)).astype(BF)
            copy_of(s, 10).start()
            copy_of(s, 7).wait_recv()
            mg2[s, 1] = (p2[s, h3, :, right].astype(F32) + rl2[s, 1].astype(F32)).astype(BF)
            copy_of(s, 11).start()

        @pl.when(t >= 4)
        def _():
            s = t - 4
            for i in (8, 9, 10, 11):
                copy_of(s, i).wait_recv()
            whole = p2[s, g].astype(F32) + ac2[s, 0].astype(F32) + ac2[s, 1].astype(F32)
            cols = pl.ds(pl.multiple_of(s * SUB, SUB), SUB)
            att_v[:, :, cols] = whole.reshape(ROWS, 2, SUB).astype(BF)

        return carry

    lax.fori_loop(0, SUBS + 4, step, 0)

    for copy in g1 + g2 + [g3, c0, w0, w1] + c1 + c2 + swaps + [c3]:
        copy.wait_send()
    for copy in list(l1.values()) + list(l2.values()):
        copy.wait_send()

    def drain(s, carry):
        for i in range(12):
            copy_of(s, i).wait_send()
        return carry

    lax.fori_loop(0, SUBS, drain, 0)


def per_device(cache, lengths, queries, fresh, w_uv, w_out, outgoing, targets):
    hbm = pl.BlockSpec(memory_space=pltpu.HBM)
    dma = pltpu.SemaphoreType.DMA
    scratch = [
        pltpu.SMEM((ROWS,), I32),
        pltpu.SMEM((MOVE,), I32),
        pltpu.SMEM((MOVE,), I32),
        pltpu.VMEM((ROWS, 2, ENT), BF),
        pltpu.VMEM((512, 512), BF),
        pltpu.VMEM((512, 512), BF),
        pltpu.VMEM((512, 512), BF),
        pltpu.VMEM((128, 128), BF),
        pltpu.VMEM((128, 128), BF),
        pltpu.VMEM((256, 512), BF),
        pltpu.VMEM((256, 512), BF),
        pltpu.VMEM((ROWS, CAP, ENT), BF),
        pltpu.VMEM((ROWS, 128, ENT), BF),
        pltpu.VMEM((4, LAT, VD), BF),
        pltpu.VMEM((512, D), BF),
        pltpu.VMEM((2, 4, 4, 32, LAT), BF),
        pltpu.VMEM((2, 4, 4, 32, LAT), BF),
        pltpu.VMEM((4, 4, 2, 32, LAT), BF),
        pltpu.VMEM((2, 256, 512), BF),
        pltpu.VMEM((2, 4, 4, 8, 128), F32),
        pltpu.VMEM((SUBS, 4, 64, SUB), BF),
        pltpu.VMEM((SUBS, 2, 32, SUB), BF),
        pltpu.VMEM((SUBS, 2, 32, SUB), BF),
        pltpu.VMEM((SUBS, 2, 64, SUB), BF),
        pltpu.VMEM((SUBS, 4, 16, SUB), BF),
        pltpu.VMEM((SUBS, 2, 16, HALF), BF),
        pltpu.VMEM((SUBS, 2, 16, HALF), BF),
        pltpu.VMEM((SUBS, 2, 16, SUB), BF),
        pltpu.VMEM((4, 2, MOVE, 32, ENT), BF),
        pltpu.VMEM((MOVE, 32, ENT), BF),
        pltpu.VMEM((3, 8, 32, ENT), BF),
        pltpu.VMEM((4, 8, 32, ENT), BF),
        pltpu.VMEM((MOVE, 32, ENT), BF),
        pltpu.VMEM((MOVE, 32, ENT), BF),
        pltpu.VMEM((40, 128), I32),
        pltpu.SMEM((40, 128), I32),
        dma((10,)),
        dma((7,)), dma((7,)),
        dma((2,)), dma((2,)),
        dma((2, 3)), dma((2, 3)),
        dma((2, 4, 3)), dma((2, 4, 3)),
        dma((4,)), dma((4,)),
        dma((SUBS, 12)), dma((SUBS, 12)),
        dma((8,)), dma((8,)),
        dma((3, 2)), dma((3, 2)),
    ]
    operands = (lengths, outgoing, targets, fresh, cache, queries.reshape(ROWS, 128, ENT), w_uv, w_out)
    new_cache, attended = pl.pallas_call(
        kernel,
        out_shape=(
            pltpu.VMEM((ROWS, CAP, ENT), BF),
            pltpu.VMEM((ROWS, 2, D), BF),
        ),
        in_specs=[hbm] * 8,
        out_specs=(pl.BlockSpec(memory_space=pltpu.VMEM), pl.BlockSpec(memory_space=pltpu.VMEM)),
        scratch_shapes=scratch,
        compiler_params=pltpu.CompilerParams(
            collective_id=0, has_side_effects=True, vmem_limit_bytes=56 * 1024 * 1024
        ),
        cost_estimate=pl.CostEstimate(flops=4 * 10**9, bytes_accessed=8 * 10**6, transcendentals=10**6),
        name="mla_decode",
    )(*[pltpu.with_memory_space_constraint(a, pltpu.HBM) for a in operands])
    return new_cache, attended


def solution(mesh):
    in_specs = (
        P(("rep", "dp"), None, None),
        P(("rep", "dp")),
        P(("rep", "dp"), None, None, None),
        P(("rep", "dp"), None, None),
        P("dp", None, None),
        P("dp", None),
        P(("rep", "dp")),
        P(("rep", "dp")),
    )
    out_specs = (P(("rep", "dp"), None, None), P(("rep", "dp"), None, None))
    return jax.shard_map(
        per_device, mesh=mesh, in_specs=in_specs, out_specs=out_specs, check_vma=False
    )
```

```python
import math

import jax
import jax.numpy as jnp
from jax import lax
from jax.experimental import pallas as pl
from jax.experimental.pallas import tpu as pltpu
from jax.sharding import PartitionSpec as P

D = 7168
LAT = 512
ENT = 576
VD = 128
ROPE = 64
CAP = 64
ROWS = 8
MOVE = 4
SUBS = 7
SUB = D // SUBS
AT = (0, 2, 4, 6)
POINT = 8
MESH = pl.DeviceIdType.MESH
BF = jnp.bfloat16
F32 = jnp.float32
I32 = jnp.int32


def iota(shape, dim):
    return lax.broadcasted_iota(I32, shape, dim)


def one_hot(mask):
    return jnp.where(mask, 1.0, 0.0).astype(BF)


def mm(a, b):
    return jnp.dot(a, b, preferred_element_type=F32)


def kernel(
    len_h, out_h, tgt_h, fresh_h, cache_h, q_h, wuv_h, wout_h,
    nc_v, att_v,
    len_s, out_s, tgt_s, fresh_v,
    turn, before, within, earlier, lower, order, flat,
    upd, q_v, wuv, wout, lat, in1, in2, vals, gall,
    part, rl, mg, ac, p2, ac2,
    cand, sib, sel, fin, swp, swr, tabv, tabs,
    lsem, gsem, grec, wsem, wrec, s1, r1, s2, r2, sv, rv,
    srs, rrs, cs, cr, cks, ckr,
):
    dp = lax.axis_index("dp")
    x, y, c = dp // 8, (dp // 2) % 4, dp % 2
    f = x + c * (y - x)
    g = y + c * (x - y)

    def dev(ff, gg, cc):
        xx = ff + c * (gg - ff)
        yy = gg + c * (ff - gg)
        return (xx * 4 + yy) * 2 + cc

    def on_f(k):
        return {"dp": dev((f + k) % 4, g, c)}

    def on_g(k):
        return {"dp": dev(f, (g + k) % 4, c)}

    sibling = {"dp": dev(f, g, 1 - c)}

    def send(src, dst, ss, rs, device):
        copy = pltpu.make_async_remote_copy(
            src_ref=src, dst_ref=dst, send_sem=ss, recv_sem=rs, device_id=device, device_id_type=MESH
        )
        copy.start()
        return copy

    small = [
        pltpu.make_async_copy(out_h, out_s, lsem.at[6]),
        pltpu.make_async_copy(tgt_h, tgt_s, lsem.at[7]),
        pltpu.make_async_copy(len_h, len_s, lsem.at[8]),
        pltpu.make_async_copy(fresh_h, fresh_v, lsem.at[9]),
    ]
    loads = [
        pltpu.make_async_copy(cache_h, upd, lsem.at[0]),
        pltpu.make_async_copy(q_h, q_v, lsem.at[1]),
        pltpu.make_async_copy(wuv_h, wuv.at[pl.ds(2 * c, 2)], lsem.at[2]),
        pltpu.make_async_copy(wout_h, wout.at[pl.ds(pl.multiple_of(256 * c, 256), 256)], lsem.at[3]),
    ]
    for load in small + loads:
        load.start()

    barrier = pltpu.get_barrier_semaphore()
    for k in (1, 2, 3):
        pl.semaphore_signal(barrier, inc=1, device_id=on_f(k), device_id_type=MESH)
        pl.semaphore_signal(barrier, inc=1, device_id=on_g(k), device_id_type=MESH)
    pl.semaphore_signal(barrier, inc=1, device_id=sibling, device_id_type=MESH)

    lane = iota((1, 128), 1)

    small[0].wait()
    small[1].wait()
    slot_lane = (lane >> 1) & 7
    dest_row = jnp.full((1, 128), -1.0, F32)
    target_row = jnp.zeros((1, 128), F32)
    for m in range(MOVE):
        goal = tgt_s[m].astype(F32)
        dest_row = jnp.where(slot_lane == out_s[m], goal, dest_row)
        target_row = jnp.where((lane & 3) == m, goal, target_row)
    row_of = iota((8, 128), 0)
    gall[c, 0, 0] = jnp.where(row_of == 0, dest_row, target_row)

    loads[0].wait()
    small[2].wait()
    small[3].wait()
    slot = iota((CAP, 1), 0)
    for r in range(ROWS):
        fresh = fresh_v[r].astype(F32)
        old = upd[r].astype(F32)
        new = jnp.where(slot == len_s[r], fresh[0:1], old)
        new = jnp.where(slot == len_s[r] + 1, fresh[1:2], new)
        upd[r] = new.astype(BF)
    mine = pl.multiple_of(c * 32, 32)
    theirs = pl.multiple_of((1 - c) * 32, 32)
    for m in range(MOVE):
        sib[m] = upd[out_s[m], pl.ds(theirs, 32)]
        cand[0, c, m] = upd[out_s[m], pl.ds(mine, 32)]

    ro = iota((512, 1), 0)
    of, og, oh, orow, ostep = ro >> 7, (ro >> 5) & 3, (ro >> 3) & 3, (ro >> 1) & 3, ro & 1
    ox = of + c * (og - of)
    oy = og + c * (of - og)
    wanted = orow * 128 + ostep * 64 + (ox * 4 + oy) * 4 + oh
    turn[...] = one_hot(iota((512, 512), 1) == wanted)


    pl.semaphore_wait(barrier, 7)
    g1 = [send(gall.at[c, 0, 0], gall.at[c, 0, k], gsem.at[k - 1], grec.at[k - 1], on_f(k)) for k in (1, 2, 3)]
    c0 = send(sib, cand.at[0, c], cs.at[0], cr.at[0], sibling)

    def pass_rows(k, sc, src):
        return send(src, cand.at[k, sc], cks.at[k - 1, sc], ckr.at[k - 1, sc], on_f(k))

    c1 = [pass_rows(k, c, cand.at[0, c]) for k in (2, 1, 3)]
    qi = iota((512, 256), 0)
    ki = iota((512, 256), 1)
    same_row = (qi >> 7) == (ki >> 6)
    ahead = (ki & 63) - ((qi >> 6) & 1)
    klane = iota((1, 256), 1) >> 6
    scale = 1.0 / math.sqrt(VD + ROPE)

    loads[1].wait()
    l1 = {}
    l2 = {}

    def onward(grp, k, block):
        for j in (1, 3, 2):
            l2[grp, k, j] = send(
                block.at[(g + j) % 4], in2.at[j, k, grp], s2.at[grp, k, j - 1], r2.at[grp, k, j - 1], on_g(j)
            )

    for grp in range(2):
        queries = q_v[4 * grp : 4 * grp + 4].reshape(512, ENT)
        keys = upd[4 * grp : 4 * grp + 4].reshape(256, ENT)
        scores = lax.dot_general(queries, keys, (((1,), (1,)), ((), ())), preferred_element_type=F32) * scale
        limit = jnp.zeros((1, 256), I32)
        for r in range(4):
            limit = jnp.where(klane == r, len_s[4 * grp + r], limit)
        scores = jnp.where(same_row & (ahead <= limit), scores, -1e30)
        weights = jnp.exp(scores - jnp.max(scores, axis=1, keepdims=True))
        probs = (weights / jnp.sum(weights, axis=1, keepdims=True)).astype(BF)
        turned = mm(turn[...], probs).astype(BF)
        latent = mm(turned, keys[:, :LAT]).astype(BF)
        lat[grp] = latent.reshape(4, 4, 32, LAT)
        for k in (2, 1, 3):
            l1[grp, k] = send(lat.at[grp, (f + k) % 4], in1.at[grp, k], s1.at[grp, k - 1], r1.at[grp, k - 1], on_f(k))
        onward(grp, 0, lat.at[grp, f])
        in2[0, 0, grp] = lat[grp, f, g]
        if grp == 0:
            c0.wait_recv()
            c1 += [pass_rows(k, 1 - c, cand.at[0, 1 - c]) for k in (2, 1, 3)]

    w0 = send(wuv_h, wuv.at[pl.ds(2 * c, 2)], wsem.at[0], wrec.at[0], sibling)
    w1 = send(wout_h, wout.at[pl.ds(pl.multiple_of(256 * c, 256), 256)], wsem.at[1], wrec.at[1], sibling)

    def source(l):
        cs_, dg_, df_ = l >> 8, (l >> 6) & 3, (l >> 4) & 3
        fs = (x + cs_ * (y - x) - df_) & 3
        gs = (y + cs_ * (x - y) - dg_) & 3
        return ((fs + cs_ * (gs - fs)) * 4 + gs + cs_ * (fs - gs)) * 2 + cs_

    wide = iota((1, 512), 1)
    tall = iota((512, 1), 0)
    from_w, from_t = source(wide), source(tall)
    slot_w, slot_t = (wide >> 1) & 7, (tall >> 1) & 7
    even = (tall & 1) == 0
    before[...] = one_hot(even & (from_t < from_w))
    within[...] = one_hot(even & (from_t == from_w) & (slot_t < slot_w))
    lt, lw = iota((128, 128), 0), iota((128, 128), 1)

    def mover(l):
        fs = (f - ((l >> 3) & 3)) & 3
        gs = (g - (l >> 5)) & 3
        return ((fs + c * (gs - fs)) * 4 + gs + c * (fs - gs)) * 2 + ((l >> 2) & 1)

    earlier[...] = one_hot(((lt >> 5) == (lw >> 5)) & (lt < lw))
    lower[...] = one_hot(mover(iota((128, 1), 0)) < mover(lane))

    for copy in g1:
        copy.wait_recv()
    g2 = [send(gall.at[c, 0], gall.at[c, k], gsem.at[2 + k], grec.at[2 + k], on_g(k)) for k in (1, 2, 3)]

    def arrived(k, sc):
        return pltpu.make_async_remote_copy(
            src_ref=cand.at[0, 0], dst_ref=cand.at[k, sc], send_sem=cks.at[k - 1, sc], recv_sem=ckr.at[k - 1, sc],
            device_id=on_f(1), device_id_type=MESH,
        )

    kept = [0] * MOVE
    count = 0
    for r in range(ROWS):
        gone = (out_s[0] == r) | (out_s[1] == r) | (out_s[2] == r) | (out_s[3] == r)
        stay = 1 - gone.astype(I32)
        for j in range(MOVE):
            kept[j] = kept[j] + jnp.where(count == j, stay * r, 0)
        count = count + stay
    for j in range(MOVE):
        nc_v[j] = upd[kept[j]]

    for copy in g2:
        copy.wait_recv()
    g3 = send(gall.at[c], gall.at[c], gsem.at[6], grec.at[6], sibling)

    def turn_corner(grp):
        for k in (1, 3, 2):
            l1[grp, k].wait_recv()
            onward(grp, k, in1.at[grp, k])
            in2[0, k, grp] = in1[grp, k, g]

    turn_corner(0)

    nr = iota((256, 1), 0)
    nf, ng = nr >> 6, (nr >> 4) & 3
    ndev = ((nf + c * (ng - nf)) * 4 + ng + c * (nf - ng)) * 2 + c
    nslot, nstep = (nr >> 1) & 7, nr & 1

    g3.wait_recv()
    rows = gall[...].reshape(32, 8, 128)
    pieces = []
    for v in range(4):
        total = jnp.zeros((1, 128), F32)
        for b in range(8):
            total = total + jnp.where((lane >> 4) == b, rows[8 * v + b][0:1], 0.0)
        pieces.append(total)
    dest_w = jnp.concatenate(pieces, axis=1).astype(I32)
    comes = dest_w == ndev
    stays = (dest_w < 0) & (from_w == ndev)
    rank_in = mm(one_hot(comes), before[...])
    rank_stay = mm(one_hot(stays), within[...])
    place = jnp.where(comes, rank_in + 4.0, jnp.where(stays, rank_stay, -1.0))
    order[...] = one_hot((place == nslot.astype(F32)) & ((wide & 1) == nstep))

    table = jnp.zeros((1, 128), F32)
    l_dg, l_df, l_sc = lane >> 5, (lane >> 3) & 3, (lane >> 2) & 1
    for sc in range(2):
        for a in range(4):
            for b in range(4):
                row = rows[sc * 16 + a * 4 + b][1:2]
                swapped = sc + c - 2 * sc * c
                la = a + swapped * (b - a)
                lb = b + swapped * (a - b)
                table = table + jnp.where((l_sc == sc) & (l_dg == la) & (l_df == lb), row, 0.0)
    table = table.astype(I32)
    tr = iota((32, 128), 0)
    tdg, tcore, tk = tr >> 3, (tr >> 2) & 1, tr & 3
    tl = iota((32, 128), 1)
    tg = (g + tdg) & 3
    tdev = ((f + c * (tg - f)) * 4 + tg + c * (f - tg)) * 2 + tcore
    hit = (table == tdev) & (tl < 32)
    nth = mm(one_hot(hit), earlier[...])
    pick = jnp.sum(jnp.where(hit & (nth == tk.astype(F32)), tl, 0), axis=1, keepdims=True)
    ur = iota((8, 128), 0)
    ucore, uj = ur >> 2, ur & 3
    udev = ((f + c * (g - f)) * 4 + g + c * (f - g)) * 2 + ucore
    own = table == udev
    spot = (lane >> 5) * 8 + ucore * 4 + mm(one_hot(own), earlier[...]).astype(I32)
    turn_in = mm(one_hot(own), lower[...])
    last = jnp.sum(jnp.where(own & (turn_in == uj.astype(F32)), spot, 0), axis=1, keepdims=True)
    tabv[0:32] = jnp.broadcast_to(pick, (32, 128))
    tabv[32:40] = jnp.broadcast_to(last, (8, 128))
    tcopy = pltpu.make_async_copy(tabv, tabs, lsem.at[4])
    tcopy.start()

    turn_corner(1)

    loads[2].wait()
    w0.wait_recv()
    def leg(j):
        return pltpu.make_async_remote_copy(
            src_ref=sel.at[j - 1], dst_ref=fin.at[j], send_sem=cs.at[3 + j], recv_sem=cr.at[3 + j],
            device_id=on_g(j), device_id_type=MESH,
        )

    def select_rows(legs):
        for j in legs:
            for i in range(8):
                which = tabs[j * 8 + i, 0]
                chosen = cand[which >> 3, (which >> 2) & 1, which & 3]
                if j:
                    sel[j - 1, i] = chosen
                else:
                    fin[0, i] = chosen
            if j:
                leg(j).start()

    tcopy.wait()
    for k in (1, 2, 3):
        for sc in range(2):
            arrived(k, sc).wait_recv()
    select_rows((1, 3, 2, 0))

    swaps = []
    for j in (0, 1, 3, 2):
        if j:
            for grp in range(2):
                for k in range(4):
                    l2[grp, k, j].wait_recv()
        block = in2[j].reshape(256, LAT)
        for h in range(4):
            value = mm(block, wuv[h]).reshape(8, 4, 8, VD)[:, h].reshape(64, VD)
            vals[c, pl.ds(64 * j, 64), pl.ds(VD * h, VD)] = value.astype(BF)
        swaps.append(
            send(vals.at[c, pl.ds(64 * j, 64)], vals.at[c, pl.ds(64 * j, 64)], sv.at[j], rv.at[j], sibling)
        )

    for copy in swaps:
        copy.wait_recv()
    flat[...] = mm(order[...], vals[...].reshape(512, 512)).astype(BF)
    loads[3].wait()
    w1.wait_recv()

    f1, f2, f3 = (f + 1) % 4, (f + 2) % 4, (f + 3) % 4
    h1, h2, h3 = (g + 1) % 4, (g + 2) % 4, (g + 3) % 4
    low, high = pl.ds(0, 32), pl.ds(32, 32)

    def rs(s, i, src, dst, device):
        return pltpu.make_async_remote_copy(
            src_ref=src, dst_ref=dst, send_sem=srs.at[s, i], recv_sem=rrs.at[s, i],
            device_id=device, device_id_type=MESH,
        )

    def copy_of(s, i):
        table = (
            lambda: rs(s, 0, part.at[s, f2, low], rl.at[s, 0], on_f(1)),
            lambda: rs(s, 1, part.at[s, f2, high], rl.at[s, 1], on_f(3)),
            lambda: rs(s, 2, part.at[s, f1, high], ac.at[s, 0, high], on_f(1)),
            lambda: rs(s, 3, part.at[s, f3, low], ac.at[s, 1, low], on_f(3)),
            lambda: rs(s, 4, mg.at[s, 0], ac.at[s, 0, low], on_f(1)),
            lambda: rs(s, 5, mg.at[s, 1], ac.at[s, 1, high], on_f(3)),
            lambda: rs(s, 6, p2.at[s, h1], ac2.at[s, 0], on_g(1)),
            lambda: rs(s, 7, p2.at[s, h2], ac2.at[s, 1], on_g(2)),
            lambda: rs(s, 8, p2.at[s, h3], ac2.at[s, 2], on_g(3)),
        )
        return table[i]()

    c3 = pltpu.make_async_remote_copy(
        src_ref=swp, dst_ref=swr, send_sem=cs.at[7], recv_sem=cr.at[7],
        device_id=sibling, device_id_type=MESH,
    )
    def place_rows():
        for j in (1, 2, 3):
            leg(j).wait_recv()
        for j in range(MOVE):
            there = tabs[32 + (1 - c) * 4 + j, 0]
            here = tabs[32 + c * 4 + j, 0]
            swp[j] = fin[there >> 3, there & 7]
            nc_v[MOVE + j, pl.ds(mine, 32)] = fin[here >> 3, here & 7]
        c3.start()

    def store_rows():
        c3.wait_recv()
        for j in range(MOVE):
            nc_v[MOVE + j, pl.ds(theirs, 32)] = swr[j]

    def step(t, carry):

        @pl.when(t < SUBS)
        def _():
            s = t
            cols = pl.ds(pl.multiple_of(s * SUB, SUB), SUB)
            part[s] = mm(flat[...], wout[:, cols]).astype(BF).reshape(4, 64, SUB)
            for i in range(4):
                copy_of(s, i).start()

        @pl.when((t >= AT[1]) & (t < SUBS + AT[1]))
        def _():
            s = t - AT[1]
            copy_of(s, 0).wait_recv()
            mg[s, 0] = (part[s, f1, low].astype(F32) + rl[s, 0].astype(F32)).astype(BF)
            copy_of(s, 4).start()
            copy_of(s, 1).wait_recv()
            mg[s, 1] = (part[s, f3, high].astype(F32) + rl[s, 1].astype(F32)).astype(BF)
            copy_of(s, 5).start()

        @pl.when((t >= AT[2]) & (t < SUBS + AT[2]))
        def _():
            s = t - AT[2]
            for i in (2, 3, 4, 5):
                copy_of(s, i).wait_recv()
            whole = part[s, f].astype(F32) + ac[s, 0].astype(F32) + ac[s, 1].astype(F32)
            p2[s] = whole.astype(BF).reshape(4, 16, SUB)
            for i in (7, 6, 8):
                copy_of(s, i).start()

        @pl.when(t >= AT[3])
        def _():
            s = t - AT[3]
            for i in (6, 7, 8):
                copy_of(s, i).wait_recv()
            whole = p2[s, g].astype(F32)
            for i in range(3):
                whole = whole + ac2[s, i].astype(F32)
            cols = pl.ds(pl.multiple_of(s * SUB, SUB), SUB)
            att_v[:, :, cols] = whole.reshape(ROWS, 2, SUB).astype(BF)

        pl.when(t == POINT)(place_rows)
        pl.when(t == POINT + 2)(store_rows)
        return carry

    lax.fori_loop(0, SUBS + AT[3], step, 0)

    for copy in g1 + g2 + [g3, c0, w0, w1] + c1 + [leg(1), leg(2), leg(3)] + swaps + [c3]:
        copy.wait_send()
    for copy in list(l1.values()) + list(l2.values()):
        copy.wait_send()

    def drain(s, carry):
        for i in range(9):
            copy_of(s, i).wait_send()
        return carry

    lax.fori_loop(0, SUBS, drain, 0)


def per_device(cache, lengths, queries, fresh, w_uv, w_out, outgoing, targets):
    hbm = pl.BlockSpec(memory_space=pltpu.HBM)
    dma = pltpu.SemaphoreType.DMA
    scratch = [
        pltpu.SMEM((ROWS,), I32),
        pltpu.SMEM((MOVE,), I32),
        pltpu.SMEM((MOVE,), I32),
        pltpu.VMEM((ROWS, 2, ENT), BF),
        pltpu.VMEM((512, 512), BF),
        pltpu.VMEM((512, 512), BF),
        pltpu.VMEM((512, 512), BF),
        pltpu.VMEM((128, 128), BF),
        pltpu.VMEM((128, 128), BF),
        pltpu.VMEM((256, 512), BF),
        pltpu.VMEM((256, 512), BF),
        pltpu.VMEM((ROWS, CAP, ENT), BF),
        pltpu.VMEM((ROWS, 128, ENT), BF),
        pltpu.VMEM((4, LAT, VD), BF),
        pltpu.VMEM((512, D), BF),
        pltpu.VMEM((2, 4, 4, 32, LAT), BF),
        pltpu.VMEM((2, 4, 4, 32, LAT), BF),
        pltpu.VMEM((4, 4, 2, 32, LAT), BF),
        pltpu.VMEM((2, 256, 512), BF),
        pltpu.VMEM((2, 4, 4, 8, 128), F32),
        pltpu.VMEM((SUBS, 4, 64, SUB), BF),
        pltpu.VMEM((SUBS, 2, 32, SUB), BF),
        pltpu.VMEM((SUBS, 2, 32, SUB), BF),
        pltpu.VMEM((SUBS, 2, 64, SUB), BF),
        pltpu.VMEM((SUBS, 4, 16, SUB), BF),
        pltpu.VMEM((SUBS, 3, 16, SUB), BF),
        pltpu.VMEM((4, 2, MOVE, 32, ENT), BF),
        pltpu.VMEM((MOVE, 32, ENT), BF),
        pltpu.VMEM((3, 8, 32, ENT), BF),
        pltpu.VMEM((4, 8, 32, ENT), BF),
        pltpu.VMEM((MOVE, 32, ENT), BF),
        pltpu.VMEM((MOVE, 32, ENT), BF),
        pltpu.VMEM((40, 128), I32),
        pltpu.SMEM((40, 128), I32),
        dma((10,)),
        dma((7,)), dma((7,)),
        dma((2,)), dma((2,)),
        dma((2, 3)), dma((2, 3)),
        dma((2, 4, 3)), dma((2, 4, 3)),
        dma((4,)), dma((4,)),
        dma((SUBS, 9)), dma((SUBS, 9)),
        dma((8,)), dma((8,)),
        dma((3, 2)), dma((3, 2)),
    ]
    operands = (lengths, outgoing, targets, fresh, cache, queries.reshape(ROWS, 128, ENT), w_uv, w_out)
    new_cache, attended = pl.pallas_call(
        kernel,
        out_shape=(
            pltpu.VMEM((ROWS, CAP, ENT), BF),
            pltpu.VMEM((ROWS, 2, D), BF),
        ),
        in_specs=[hbm] * 8,
        out_specs=(pl.BlockSpec(memory_space=pltpu.VMEM), pl.BlockSpec(memory_space=pltpu.VMEM)),
        scratch_shapes=scratch,
        compiler_params=pltpu.CompilerParams(
            collective_id=0, has_side_effects=True, vmem_limit_bytes=56 * 1024 * 1024
        ),
        cost_estimate=pl.CostEstimate(flops=4 * 10**9, bytes_accessed=8 * 10**6, transcendentals=10**6),
        name="mla_decode",
    )(*[pltpu.with_memory_space_constraint(a, pltpu.HBM) for a in operands])
    return new_cache, attended


def solution(mesh):
    in_specs = (
        P(("rep", "dp"), None, None),
        P(("rep", "dp")),
        P(("rep", "dp"), None, None, None),
        P(("rep", "dp"), None, None),
        P("dp", None, None),
        P("dp", None),
        P(("rep", "dp")),
        P(("rep", "dp")),
    )
    out_specs = (P(("rep", "dp"), None, None), P(("rep", "dp"), None, None))
    return jax.shard_map(
        per_device, mesh=mesh, in_specs=in_specs, out_specs=out_specs, check_vma=False
    )
```

```python
import math

import jax
import jax.numpy as jnp
from jax import lax
from jax.experimental import pallas as pl
from jax.experimental.pallas import tpu as pltpu
from jax.sharding import PartitionSpec as P

D = 7168
LAT = 512
ENT = 576
VD = 128
ROPE = 64
CAP = 64
ROWS = 8
MOVE = 4
SUBS = 7
SUB = D // SUBS
AT = (0, 2, 4, 6)
POINT = 8
MESH = pl.DeviceIdType.MESH
BF = jnp.bfloat16
F32 = jnp.float32
I32 = jnp.int32


def iota(shape, dim):
    return lax.broadcasted_iota(I32, shape, dim)


def one_hot(mask):
    return jnp.where(mask, 1.0, 0.0).astype(BF)


def mm(a, b):
    return jnp.dot(a, b, preferred_element_type=F32)


def kernel(
    len_h, out_h, tgt_h, fresh_h, cache_h, q_h, wuv_h, wout_h,
    nc_v, att_v,
    len_s, out_s, tgt_s, fresh_v,
    turn, before, within, earlier, lower, order, flat,
    upd, q_v, wuv, wout, lat, in1, in2, vals, gall,
    part, rl, mg, ac, p2, ac2,
    cand, sib, sel, fin, swp, swr, tabv, tabs,
    lsem, gsem, grec, wsem, wrec, s1, r1, s2, r2, sv, rv,
    srs, rrs, cs, cr, cks, ckr,
):
    dp = lax.axis_index("dp")
    x, y, c = dp // 8, (dp // 2) % 4, dp % 2
    f = x + c * (y - x)
    g = y + c * (x - y)

    def dev(ff, gg, cc):
        xx = ff + c * (gg - ff)
        yy = gg + c * (ff - gg)
        return (xx * 4 + yy) * 2 + cc

    def on_f(k):
        return {"dp": dev((f + k) % 4, g, c)}

    def on_g(k):
        return {"dp": dev(f, (g + k) % 4, c)}

    sibling = {"dp": dev(f, g, 1 - c)}

    def send(src, dst, ss, rs, device):
        copy = pltpu.make_async_remote_copy(
            src_ref=src, dst_ref=dst, send_sem=ss, recv_sem=rs, device_id=device, device_id_type=MESH
        )
        copy.start()
        return copy

    small = [
        pltpu.make_async_copy(out_h, out_s, lsem.at[6]),
        pltpu.make_async_copy(tgt_h, tgt_s, lsem.at[7]),
        pltpu.make_async_copy(len_h, len_s, lsem.at[8]),
        pltpu.make_async_copy(fresh_h, fresh_v, lsem.at[9]),
    ]
    loads = [
        pltpu.make_async_copy(cache_h, upd, lsem.at[0]),
        pltpu.make_async_copy(q_h, q_v, lsem.at[1]),
        pltpu.make_async_copy(wuv_h, wuv.at[pl.ds(2 * c, 2)], lsem.at[2]),
        pltpu.make_async_copy(wout_h, wout.at[pl.ds(pl.multiple_of(256 * c, 256), 256)], lsem.at[3]),
    ]
    for load in small + loads:
        load.start()

    barrier = pltpu.get_barrier_semaphore()
    for k in (1, 2, 3):
        pl.semaphore_signal(barrier, inc=1, device_id=on_f(k), device_id_type=MESH)
        pl.semaphore_signal(barrier, inc=1, device_id=on_g(k), device_id_type=MESH)
    pl.semaphore_signal(barrier, inc=1, device_id=sibling, device_id_type=MESH)

    lane = iota((1, 128), 1)

    small[0].wait()
    small[1].wait()
    slot_lane = (lane >> 1) & 7
    dest_row = jnp.full((1, 128), -1.0, F32)
    target_row = jnp.zeros((1, 128), F32)
    for m in range(MOVE):
        goal = tgt_s[m].astype(F32)
        dest_row = jnp.where(slot_lane == out_s[m], goal, dest_row)
        target_row = jnp.where((lane & 3) == m, goal, target_row)
    row_of = iota((8, 128), 0)
    gall[c, 0, 0] = jnp.where(row_of == 0, dest_row, target_row)

    loads[0].wait()
    small[2].wait()
    small[3].wait()
    slot = iota((CAP, 1), 0)
    for r in range(ROWS):
        fresh = fresh_v[r].astype(F32)
        old = upd[r].astype(F32)
        new = jnp.where(slot == len_s[r], fresh[0:1], old)
        new = jnp.where(slot == len_s[r] + 1, fresh[1:2], new)
        upd[r] = new.astype(BF)
    mine = pl.multiple_of(c * 32, 32)
    theirs = pl.multiple_of((1 - c) * 32, 32)
    for m in range(MOVE):
        sib[m] = upd[out_s[m], pl.ds(theirs, 32)]
        cand[0, c, m] = upd[out_s[m], pl.ds(mine, 32)]

    ro = iota((512, 1), 0)
    of, og, oh, orow, ostep = ro >> 7, (ro >> 5) & 3, (ro >> 3) & 3, (ro >> 1) & 3, ro & 1
    ox = of + c * (og - of)
    oy = og + c * (of - og)
    wanted = orow * 128 + ostep * 64 + (ox * 4 + oy) * 4 + oh
    turn[...] = one_hot(iota((512, 512), 1) == wanted)


    pl.semaphore_wait(barrier, 7)
    g1 = [send(gall.at[c, 0, 0], gall.at[c, 0, k], gsem.at[k - 1], grec.at[k - 1], on_f(k)) for k in (1, 2, 3)]
    c0 = send(sib, cand.at[0, c], cs.at[0], cr.at[0], sibling)

    def pass_rows(k, sc, src):
        return send(src, cand.at[k, sc], cks.at[k - 1, sc], ckr.at[k - 1, sc], on_f(k))

    c1 = [pass_rows(k, c, cand.at[0, c]) for k in (2, 1, 3)]
    qi = iota((512, 256), 0)
    ki = iota((512, 256), 1)
    same_row = (qi >> 7) == (ki >> 6)
    ahead = (ki & 63) - ((qi >> 6) & 1)
    klane = iota((1, 256), 1) >> 6
    scale = 1.0 / math.sqrt(VD + ROPE)

    loads[1].wait()
    l1 = {}
    l2 = {}

    def onward(grp, k, block):
        for j in (1, 3, 2):
            l2[grp, k, j] = send(
                block.at[(g + j) % 4], in2.at[j, k, grp], s2.at[grp, k, j - 1], r2.at[grp, k, j - 1], on_g(j)
            )

    for grp in range(2):
        queries = q_v[4 * grp : 4 * grp + 4].reshape(512, ENT)
        keys = upd[4 * grp : 4 * grp + 4].reshape(256, ENT)
        scores = lax.dot_general(queries, keys, (((1,), (1,)), ((), ())), preferred_element_type=F32) * scale
        limit = jnp.zeros((1, 256), I32)
        for r in range(4):
            limit = jnp.where(klane == r, len_s[4 * grp + r], limit)
        scores = jnp.where(same_row & (ahead <= limit), scores, -1e30)
        weights = jnp.exp(scores - jnp.max(scores, axis=1, keepdims=True))
        probs = (weights / jnp.sum(weights, axis=1, keepdims=True)).astype(BF)
        turned = mm(turn[...], probs).astype(BF)
        latent = mm(turned, keys[:, :LAT]).astype(BF)
        lat[grp] = latent.reshape(4, 4, 32, LAT)
        for k in (2, 1, 3):
            l1[grp, k] = send(lat.at[grp, (f + k) % 4], in1.at[grp, k], s1.at[grp, k - 1], r1.at[grp, k - 1], on_f(k))
        onward(grp, 0, lat.at[grp, f])
        in2[0, 0, grp] = lat[grp, f, g]
        if grp == 0:
            c0.wait_recv()
            c1 += [pass_rows(k, 1 - c, cand.at[0, 1 - c]) for k in (2, 1, 3)]

    w0 = send(wuv_h, wuv.at[pl.ds(2 * c, 2)], wsem.at[0], wrec.at[0], sibling)
    w1 = send(wout_h, wout.at[pl.ds(pl.multiple_of(256 * c, 256), 256)], wsem.at[1], wrec.at[1], sibling)

    def source(l):
        cs_, dg_, df_ = l >> 8, (l >> 6) & 3, (l >> 4) & 3
        fs = (x + cs_ * (y - x) - df_) & 3
        gs = (y + cs_ * (x - y) - dg_) & 3
        return ((fs + cs_ * (gs - fs)) * 4 + gs + cs_ * (fs - gs)) * 2 + cs_

    wide = iota((1, 512), 1)
    tall = iota((512, 1), 0)
    from_w, from_t = source(wide), source(tall)
    slot_w, slot_t = (wide >> 1) & 7, (tall >> 1) & 7
    even = (tall & 1) == 0
    before[...] = one_hot(even & (from_t < from_w))
    within[...] = one_hot(even & (from_t == from_w) & (slot_t < slot_w))
    lt, lw = iota((128, 128), 0), iota((128, 128), 1)

    def mover(l):
        fs = (f - ((l >> 3) & 3)) & 3
        gs = (g - (l >> 5)) & 3
        return ((fs + c * (gs - fs)) * 4 + gs + c * (fs - gs)) * 2 + ((l >> 2) & 1)

    earlier[...] = one_hot(((lt >> 5) == (lw >> 5)) & (lt < lw))
    lower[...] = one_hot(mover(iota((128, 1), 0)) < mover(lane))

    for copy in g1:
        copy.wait_recv()
    g2 = [send(gall.at[c, 0], gall.at[c, k], gsem.at[2 + k], grec.at[2 + k], on_g(k)) for k in (1, 2, 3)]

    def arrived(k, sc):
        return pltpu.make_async_remote_copy(
            src_ref=cand.at[0, 0], dst_ref=cand.at[k, sc], send_sem=cks.at[k - 1, sc], recv_sem=ckr.at[k - 1, sc],
            device_id=on_f(1), device_id_type=MESH,
        )

    kept = [0] * MOVE
    count = 0
    for r in range(ROWS):
        gone = (out_s[0] == r) | (out_s[1] == r) | (out_s[2] == r) | (out_s[3] == r)
        stay = 1 - gone.astype(I32)
        for j in range(MOVE):
            kept[j] = kept[j] + jnp.where(count == j, stay * r, 0)
        count = count + stay
    for j in range(MOVE):
        nc_v[j] = upd[kept[j]]

    for copy in g2:
        copy.wait_recv()
    g3 = send(gall.at[c], gall.at[c], gsem.at[6], grec.at[6], sibling)

    def turn_corner(grp):
        for k in (1, 3, 2):
            l1[grp, k].wait_recv()
            onward(grp, k, in1.at[grp, k])
            in2[0, k, grp] = in1[grp, k, g]

    turn_corner(0)

    nr = iota((256, 1), 0)
    nf, ng = nr >> 6, (nr >> 4) & 3
    ndev = ((nf + c * (ng - nf)) * 4 + ng + c * (nf - ng)) * 2 + c
    nslot, nstep = (nr >> 1) & 7, nr & 1

    g3.wait_recv()
    rows = gall[...].reshape(32, 8, 128)
    pieces = []
    for v in range(4):
        total = jnp.zeros((1, 128), F32)
        for b in range(8):
            total = total + jnp.where((lane >> 4) == b, rows[8 * v + b][0:1], 0.0)
        pieces.append(total)
    dest_w = jnp.concatenate(pieces, axis=1).astype(I32)
    comes = dest_w == ndev
    stays = (dest_w < 0) & (from_w == ndev)
    rank_in = mm(one_hot(comes), before[...])
    rank_stay = mm(one_hot(stays), within[...])
    place = jnp.where(comes, rank_in + 4.0, jnp.where(stays, rank_stay, -1.0))
    order[...] = one_hot((place == nslot.astype(F32)) & ((wide & 1) == nstep))

    table = jnp.zeros((1, 128), F32)
    l_dg, l_df, l_sc = lane >> 5, (lane >> 3) & 3, (lane >> 2) & 1
    for sc in range(2):
        for a in range(4):
            for b in range(4):
                row = rows[sc * 16 + a * 4 + b][1:2]
                swapped = sc + c - 2 * sc * c
                la = a + swapped * (b - a)
                lb = b + swapped * (a - b)
                table = table + jnp.where((l_sc == sc) & (l_dg == la) & (l_df == lb), row, 0.0)
    table = table.astype(I32)
    tr = iota((32, 128), 0)
    tdg, tcore, tk = tr >> 3, (tr >> 2) & 1, tr & 3
    tl = iota((32, 128), 1)
    tg = (g + tdg) & 3
    tdev = ((f + c * (tg - f)) * 4 + tg + c * (f - tg)) * 2 + tcore
    hit = (table == tdev) & (tl < 32)
    nth = mm(one_hot(hit), earlier[...])
    pick = jnp.sum(jnp.where(hit & (nth == tk.astype(F32)), tl, 0), axis=1, keepdims=True)
    ur = iota((8, 128), 0)
    ucore, uj = ur >> 2, ur & 3
    udev = ((f + c * (g - f)) * 4 + g + c * (f - g)) * 2 + ucore
    own = table == udev
    spot = (lane >> 5) * 8 + ucore * 4 + mm(one_hot(own), earlier[...]).astype(I32)
    turn_in = mm(one_hot(own), lower[...])
    last = jnp.sum(jnp.where(own & (turn_in == uj.astype(F32)), spot, 0), axis=1, keepdims=True)
    tabv[0:32] = jnp.broadcast_to(pick, (32, 128))
    tabv[32:40] = jnp.broadcast_to(last, (8, 128))
    tcopy = pltpu.make_async_copy(tabv, tabs, lsem.at[4])
    tcopy.start()

    turn_corner(1)

    loads[2].wait()
    w0.wait_recv()
    def leg(j):
        return pltpu.make_async_remote_copy(
            src_ref=sel.at[j - 1], dst_ref=fin.at[j], send_sem=cs.at[3 + j], recv_sem=cr.at[3 + j],
            device_id=on_g(j), device_id_type=MESH,
        )

    def select_rows(legs):
        for j in legs:
            for i in range(8):
                which = tabs[j * 8 + i, 0]
                chosen = cand[which >> 3, (which >> 2) & 1, which & 3]
                if j:
                    sel[j - 1, i] = chosen
                else:
                    fin[0, i] = chosen
            if j:
                leg(j).start()

    tcopy.wait()
    for k in (1, 2, 3):
        for sc in range(2):
            arrived(k, sc).wait_recv()
    select_rows((2, 1, 3, 0))

    swaps = []
    for j in (0, 1, 3, 2):
        if j:
            for grp in range(2):
                for k in range(4):
                    l2[grp, k, j].wait_recv()
        block = in2[j].reshape(256, LAT)
        for h in range(4):
            value = mm(block, wuv[h]).reshape(8, 4, 8, VD)[:, h].reshape(64, VD)
            vals[c, pl.ds(64 * j, 64), pl.ds(VD * h, VD)] = value.astype(BF)
        swaps.append(
            send(vals.at[c, pl.ds(64 * j, 64)], vals.at[c, pl.ds(64 * j, 64)], sv.at[j], rv.at[j], sibling)
        )

    for copy in swaps:
        copy.wait_recv()
    flat[...] = mm(order[...], vals[...].reshape(512, 512)).astype(BF)
    loads[3].wait()
    w1.wait_recv()

    f1, f2, f3 = (f + 1) % 4, (f + 2) % 4, (f + 3) % 4
    h1, h2, h3 = (g + 1) % 4, (g + 2) % 4, (g + 3) % 4
    low, high = pl.ds(0, 32), pl.ds(32, 32)

    def rs(s, i, src, dst, device):
        return pltpu.make_async_remote_copy(
            src_ref=src, dst_ref=dst, send_sem=srs.at[s, i], recv_sem=rrs.at[s, i],
            device_id=device, device_id_type=MESH,
        )

    def copy_of(s, i):
        table = (
            lambda: rs(s, 0, part.at[s, f2, low], rl.at[s, 0], on_f(1)),
            lambda: rs(s, 1, part.at[s, f2, high], rl.at[s, 1], on_f(3)),
            lambda: rs(s, 2, part.at[s, f1, high], ac.at[s, 0, high], on_f(1)),
            lambda: rs(s, 3, part.at[s, f3, low], ac.at[s, 1, low], on_f(3)),
            lambda: rs(s, 4, mg.at[s, 0], ac.at[s, 0, low], on_f(1)),
            lambda: rs(s, 5, mg.at[s, 1], ac.at[s, 1, high], on_f(3)),
            lambda: rs(s, 6, p2.at[s, h1], ac2.at[s, 0], on_g(1)),
            lambda: rs(s, 7, p2.at[s, h2], ac2.at[s, 1], on_g(2)),
            lambda: rs(s, 8, p2.at[s, h3], ac2.at[s, 2], on_g(3)),
        )
        return table[i]()

    c3 = pltpu.make_async_remote_copy(
        src_ref=swp, dst_ref=swr, send_sem=cs.at[7], recv_sem=cr.at[7],
        device_id=sibling, device_id_type=MESH,
    )
    def place_rows():
        for j in (1, 2, 3):
            leg(j).wait_recv()
        for j in range(MOVE):
            there = tabs[32 + (1 - c) * 4 + j, 0]
            here = tabs[32 + c * 4 + j, 0]
            swp[j] = fin[there >> 3, there & 7]
            nc_v[MOVE + j, pl.ds(mine, 32)] = fin[here >> 3, here & 7]
        c3.start()

    def store_rows():
        c3.wait_recv()
        for j in range(MOVE):
            nc_v[MOVE + j, pl.ds(theirs, 32)] = swr[j]

    def step(t, carry):

        @pl.when(t < SUBS)
        def _():
            s = t
            cols = pl.ds(pl.multiple_of(s * SUB, SUB), SUB)
            part[s] = mm(flat[...], wout[:, cols]).astype(BF).reshape(4, 64, SUB)
            for i in range(4):
                copy_of(s, i).start()

        @pl.when((t >= AT[1]) & (t < SUBS + AT[1]))
        def _():
            s = t - AT[1]
            copy_of(s, 0).wait_recv()
            mg[s, 0] = (part[s, f1, low].astype(F32) + rl[s, 0].astype(F32)).astype(BF)
            copy_of(s, 4).start()
            copy_of(s, 1).wait_recv()
            mg[s, 1] = (part[s, f3, high].astype(F32) + rl[s, 1].astype(F32)).astype(BF)
            copy_of(s, 5).start()

        @pl.when((t >= AT[2]) & (t < SUBS + AT[2]))
        def _():
            s = t - AT[2]
            for i in (2, 3, 4, 5):
                copy_of(s, i).wait_recv()
            whole = part[s, f].astype(F32) + ac[s, 0].astype(F32) + ac[s, 1].astype(F32)
            p2[s] = whole.astype(BF).reshape(4, 16, SUB)
            for i in (7, 6, 8):
                copy_of(s, i).start()

        @pl.when(t >= AT[3])
        def _():
            s = t - AT[3]
            for i in (6, 7, 8):
                copy_of(s, i).wait_recv()
            whole = p2[s, g].astype(F32)
            for i in range(3):
                whole = whole + ac2[s, i].astype(F32)
            cols = pl.ds(pl.multiple_of(s * SUB, SUB), SUB)
            att_v[:, :, cols] = whole.reshape(ROWS, 2, SUB).astype(BF)

        pl.when(t == POINT)(place_rows)
        pl.when(t == POINT + 2)(store_rows)
        return carry

    lax.fori_loop(0, SUBS + AT[3], step, 0)

    for copy in g1 + g2 + [g3, c0, w0, w1] + c1 + [leg(1), leg(2), leg(3)] + swaps + [c3]:
        copy.wait_send()
    for copy in list(l1.values()) + list(l2.values()):
        copy.wait_send()

    def drain(s, carry):
        for i in range(9):
            copy_of(s, i).wait_send()
        return carry

    lax.fori_loop(0, SUBS, drain, 0)


def per_device(cache, lengths, queries, fresh, w_uv, w_out, outgoing, targets):
    hbm = pl.BlockSpec(memory_space=pltpu.HBM)
    dma = pltpu.SemaphoreType.DMA
    scratch = [
        pltpu.SMEM((ROWS,), I32),
        pltpu.SMEM((MOVE,), I32),
        pltpu.SMEM((MOVE,), I32),
        pltpu.VMEM((ROWS, 2, ENT), BF),
        pltpu.VMEM((512, 512), BF),
        pltpu.VMEM((512, 512), BF),
        pltpu.VMEM((512, 512), BF),
        pltpu.VMEM((128, 128), BF),
        pltpu.VMEM((128, 128), BF),
        pltpu.VMEM((256, 512), BF),
        pltpu.VMEM((256, 512), BF),
        pltpu.VMEM((ROWS, CAP, ENT), BF),
        pltpu.VMEM((ROWS, 128, ENT), BF),
        pltpu.VMEM((4, LAT, VD), BF),
        pltpu.VMEM((512, D), BF),
        pltpu.VMEM((2, 4, 4, 32, LAT), BF),
        pltpu.VMEM((2, 4, 4, 32, LAT), BF),
        pltpu.VMEM((4, 4, 2, 32, LAT), BF),
        pltpu.VMEM((2, 256, 512), BF),
        pltpu.VMEM((2, 4, 4, 8, 128), F32),
        pltpu.VMEM((SUBS, 4, 64, SUB), BF),
        pltpu.VMEM((SUBS, 2, 32, SUB), BF),
        pltpu.VMEM((SUBS, 2, 32, SUB), BF),
        pltpu.VMEM((SUBS, 2, 64, SUB), BF),
        pltpu.VMEM((SUBS, 4, 16, SUB), BF),
        pltpu.VMEM((SUBS, 3, 16, SUB), BF),
        pltpu.VMEM((4, 2, MOVE, 32, ENT), BF),
        pltpu.VMEM((MOVE, 32, ENT), BF),
        pltpu.VMEM((3, 8, 32, ENT), BF),
        pltpu.VMEM((4, 8, 32, ENT), BF),
        pltpu.VMEM((MOVE, 32, ENT), BF),
        pltpu.VMEM((MOVE, 32, ENT), BF),
        pltpu.VMEM((40, 128), I32),
        pltpu.SMEM((40, 128), I32),
        dma((10,)),
        dma((7,)), dma((7,)),
        dma((2,)), dma((2,)),
        dma((2, 3)), dma((2, 3)),
        dma((2, 4, 3)), dma((2, 4, 3)),
        dma((4,)), dma((4,)),
        dma((SUBS, 9)), dma((SUBS, 9)),
        dma((8,)), dma((8,)),
        dma((3, 2)), dma((3, 2)),
    ]
    operands = (lengths, outgoing, targets, fresh, cache, queries.reshape(ROWS, 128, ENT), w_uv, w_out)
    new_cache, attended = pl.pallas_call(
        kernel,
        out_shape=(
            pltpu.VMEM((ROWS, CAP, ENT), BF),
            pltpu.VMEM((ROWS, 2, D), BF),
        ),
        in_specs=[hbm] * 8,
        out_specs=(pl.BlockSpec(memory_space=pltpu.VMEM), pl.BlockSpec(memory_space=pltpu.VMEM)),
        scratch_shapes=scratch,
        compiler_params=pltpu.CompilerParams(
            collective_id=0, has_side_effects=True, vmem_limit_bytes=56 * 1024 * 1024
        ),
        cost_estimate=pl.CostEstimate(flops=4 * 10**9, bytes_accessed=8 * 10**6, transcendentals=10**6),
        name="mla_decode",
    )(*[pltpu.with_memory_space_constraint(a, pltpu.HBM) for a in operands])
    return new_cache, attended


def solution(mesh):
    in_specs = (
        P(("rep", "dp"), None, None),
        P(("rep", "dp")),
        P(("rep", "dp"), None, None, None),
        P(("rep", "dp"), None, None),
        P("dp", None, None),
        P("dp", None),
        P(("rep", "dp")),
        P(("rep", "dp")),
    )
    out_specs = (P(("rep", "dp"), None, None), P(("rep", "dp"), None, None))
    return jax.shard_map(
        per_device, mesh=mesh, in_specs=in_specs, out_specs=out_specs, check_vma=False
    )
```

```python
import math

import jax
import jax.numpy as jnp
from jax import lax
from jax.experimental import pallas as pl
from jax.experimental.pallas import tpu as pltpu
from jax.sharding import PartitionSpec as P

D = 7168
LAT = 512
ENT = 576
VD = 128
ROPE = 64
CAP = 64
ROWS = 8
MOVE = 4
SUBS = 7
SUB = D // SUBS
AT = (0, 2, 4, 6)
POINT = 8
MESH = pl.DeviceIdType.MESH
BF = jnp.bfloat16
F32 = jnp.float32
I32 = jnp.int32


def iota(shape, dim):
    return lax.broadcasted_iota(I32, shape, dim)


def one_hot(mask):
    return jnp.where(mask, 1.0, 0.0).astype(BF)


def mm(a, b):
    return jnp.dot(a, b, preferred_element_type=F32)


def kernel(
    len_h, out_h, tgt_h, fresh_h, cache_h, q_h, wuv_h, wout_h,
    nc_v, att_v,
    len_s, out_s, tgt_s, fresh_v,
    turn, before, within, earlier, lower, order, flat,
    upd, q_v, wuv, wout, lat, in1, in2, vals, gall,
    part, rl, mg, ac, p2, ac2,
    cand, sib, sel, fin, swp, swr, tabv, tabs,
    lsem, gsem, grec, wsem, wrec, s1, r1, s2, r2, sv, rv,
    srs, rrs, cs, cr, cks, ckr,
):
    dp = lax.axis_index("dp")
    x, y, c = dp // 8, (dp // 2) % 4, dp % 2
    f = x + c * (y - x)
    g = y + c * (x - y)

    def dev(ff, gg, cc):
        xx = ff + c * (gg - ff)
        yy = gg + c * (ff - gg)
        return (xx * 4 + yy) * 2 + cc

    def on_f(k):
        return {"dp": dev((f + k) % 4, g, c)}

    def on_g(k):
        return {"dp": dev(f, (g + k) % 4, c)}

    sibling = {"dp": dev(f, g, 1 - c)}

    def send(src, dst, ss, rs, device):
        copy = pltpu.make_async_remote_copy(
            src_ref=src, dst_ref=dst, send_sem=ss, recv_sem=rs, device_id=device, device_id_type=MESH
        )
        copy.start()
        return copy

    small = [
        pltpu.make_async_copy(out_h, out_s, lsem.at[6]),
        pltpu.make_async_copy(tgt_h, tgt_s, lsem.at[7]),
        pltpu.make_async_copy(len_h, len_s, lsem.at[8]),
        pltpu.make_async_copy(fresh_h, fresh_v, lsem.at[9]),
    ]
    loads = [
        pltpu.make_async_copy(cache_h, upd, lsem.at[0]),
        pltpu.make_async_copy(q_h, q_v, lsem.at[1]),
        pltpu.make_async_copy(wuv_h, wuv.at[pl.ds(2 * c, 2)], lsem.at[2]),
        pltpu.make_async_copy(wout_h, wout.at[pl.ds(pl.multiple_of(256 * c, 256), 256)], lsem.at[3]),
    ]
    for load in small + loads:
        load.start()

    barrier = pltpu.get_barrier_semaphore()
    for k in (1, 2, 3):
        pl.semaphore_signal(barrier, inc=1, device_id=on_f(k), device_id_type=MESH)
        pl.semaphore_signal(barrier, inc=1, device_id=on_g(k), device_id_type=MESH)
    pl.semaphore_signal(barrier, inc=1, device_id=sibling, device_id_type=MESH)

    lane = iota((1, 128), 1)

    small[0].wait()
    small[1].wait()
    slot_lane = (lane >> 1) & 7
    dest_row = jnp.full((1, 128), -1.0, F32)
    target_row = jnp.zeros((1, 128), F32)
    for m in range(MOVE):
        goal = tgt_s[m].astype(F32)
        dest_row = jnp.where(slot_lane == out_s[m], goal, dest_row)
        target_row = jnp.where((lane & 3) == m, goal, target_row)
    row_of = iota((8, 128), 0)
    gall[c, 0, 0] = jnp.where(row_of == 0, dest_row, target_row)

    loads[0].wait()
    small[2].wait()
    small[3].wait()
    slot = iota((CAP, 1), 0)
    for r in range(ROWS):
        fresh = fresh_v[r].astype(F32)
        old = upd[r].astype(F32)
        new = jnp.where(slot == len_s[r], fresh[0:1], old)
        new = jnp.where(slot == len_s[r] + 1, fresh[1:2], new)
        upd[r] = new.astype(BF)
    mine = pl.multiple_of(c * 32, 32)
    theirs = pl.multiple_of((1 - c) * 32, 32)
    for m in range(MOVE):
        sib[m] = upd[out_s[m], pl.ds(theirs, 32)]
        cand[0, c, m] = upd[out_s[m], pl.ds(mine, 32)]

    ro = iota((512, 1), 0)
    of, og, oh, orow, ostep = ro >> 7, (ro >> 5) & 3, (ro >> 3) & 3, (ro >> 1) & 3, ro & 1
    ox = of + c * (og - of)
    oy = og + c * (of - og)
    wanted = orow * 128 + ostep * 64 + (ox * 4 + oy) * 4 + oh
    turn[...] = one_hot(iota((512, 512), 1) == wanted)


    pl.semaphore_wait(barrier, 7)
    g1 = [send(gall.at[c, 0, 0], gall.at[c, 0, k], gsem.at[k - 1], grec.at[k - 1], on_f(k)) for k in (1, 2, 3)]
    c0 = send(sib, cand.at[0, c], cs.at[0], cr.at[0], sibling)

    def pass_rows(k, sc, src):
        return send(src, cand.at[k, sc], cks.at[k - 1, sc], ckr.at[k - 1, sc], on_f(k))

    c1 = [pass_rows(k, c, cand.at[0, c]) for k in (2, 1, 3)]
    qi = iota((512, 256), 0)
    ki = iota((512, 256), 1)
    same_row = (qi >> 7) == (ki >> 6)
    ahead = (ki & 63) - ((qi >> 6) & 1)
    klane = iota((1, 256), 1) >> 6
    scale = 1.0 / math.sqrt(VD + ROPE)

    loads[1].wait()
    l1 = {}
    l2 = {}

    def onward(grp, k, block):
        for j in (1, 3, 2):
            l2[grp, k, j] = send(
                block.at[(g + j) % 4], in2.at[j, k, grp], s2.at[grp, k, j - 1], r2.at[grp, k, j - 1], on_g(j)
            )

    for grp in range(2):
        queries = q_v[4 * grp : 4 * grp + 4].reshape(512, ENT)
        keys = upd[4 * grp : 4 * grp + 4].reshape(256, ENT)
        scores = lax.dot_general(queries, keys, (((1,), (1,)), ((), ())), preferred_element_type=F32) * scale
        limit = jnp.zeros((1, 256), I32)
        for r in range(4):
            limit = jnp.where(klane == r, len_s[4 * grp + r], limit)
        scores = jnp.where(same_row & (ahead <= limit), scores, -1e30)
        weights = jnp.exp(scores - jnp.max(scores, axis=1, keepdims=True))
        probs = (weights / jnp.sum(weights, axis=1, keepdims=True)).astype(BF)
        turned = mm(turn[...], probs).astype(BF)
        latent = mm(turned, keys[:, :LAT]).astype(BF)
        lat[grp] = latent.reshape(4, 4, 32, LAT)
        for k in (1, 3, 2):
            l1[grp, k] = send(lat.at[grp, (f + k) % 4], in1.at[grp, k], s1.at[grp, k - 1], r1.at[grp, k - 1], on_f(k))
        onward(grp, 0, lat.at[grp, f])
        in2[0, 0, grp] = lat[grp, f, g]
        if grp == 0:
            c0.wait_recv()
            c1 += [pass_rows(k, 1 - c, cand.at[0, 1 - c]) for k in (2, 1, 3)]

    w0 = send(wuv_h, wuv.at[pl.ds(2 * c, 2)], wsem.at[0], wrec.at[0], sibling)
    w1 = send(wout_h, wout.at[pl.ds(pl.multiple_of(256 * c, 256), 256)], wsem.at[1], wrec.at[1], sibling)

    def source(l):
        cs_, dg_, df_ = l >> 8, (l >> 6) & 3, (l >> 4) & 3
        fs = (x + cs_ * (y - x) - df_) & 3
        gs = (y + cs_ * (x - y) - dg_) & 3
        return ((fs + cs_ * (gs - fs)) * 4 + gs + cs_ * (fs - gs)) * 2 + cs_

    wide = iota((1, 512), 1)
    tall = iota((512, 1), 0)
    from_w, from_t = source(wide), source(tall)
    slot_w, slot_t = (wide >> 1) & 7, (tall >> 1) & 7
    even = (tall & 1) == 0
    before[...] = one_hot(even & (from_t < from_w))
    within[...] = one_hot(even & (from_t == from_w) & (slot_t < slot_w))
    lt, lw = iota((128, 128), 0), iota((128, 128), 1)

    def mover(l):
        fs = (f - ((l >> 3) & 3)) & 3
        gs = (g - (l >> 5)) & 3
        return ((fs + c * (gs - fs)) * 4 + gs + c * (fs - gs)) * 2 + ((l >> 2) & 1)

    earlier[...] = one_hot(((lt >> 5) == (lw >> 5)) & (lt < lw))
    lower[...] = one_hot(mover(iota((128, 1), 0)) < mover(lane))

    for copy in g1:
        copy.wait_recv()
    g2 = [send(gall.at[c, 0], gall.at[c, k], gsem.at[2 + k], grec.at[2 + k], on_g(k)) for k in (1, 2, 3)]

    def arrived(k, sc):
        return pltpu.make_async_remote_copy(
            src_ref=cand.at[0, 0], dst_ref=cand.at[k, sc], send_sem=cks.at[k - 1, sc], recv_sem=ckr.at[k - 1, sc],
            device_id=on_f(1), device_id_type=MESH,
        )

    kept = [0] * MOVE
    count = 0
    for r in range(ROWS):
        gone = (out_s[0] == r) | (out_s[1] == r) | (out_s[2] == r) | (out_s[3] == r)
        stay = 1 - gone.astype(I32)
        for j in range(MOVE):
            kept[j] = kept[j] + jnp.where(count == j, stay * r, 0)
        count = count + stay
    for j in range(MOVE):
        nc_v[j] = upd[kept[j]]

    for copy in g2:
        copy.wait_recv()
    g3 = send(gall.at[c], gall.at[c], gsem.at[6], grec.at[6], sibling)

    def turn_corner(grp):
        for k in (1, 3, 2):
            l1[grp, k].wait_recv()
            onward(grp, k, in1.at[grp, k])
            in2[0, k, grp] = in1[grp, k, g]

    turn_corner(0)

    nr = iota((256, 1), 0)
    nf, ng = nr >> 6, (nr >> 4) & 3
    ndev = ((nf + c * (ng - nf)) * 4 + ng + c * (nf - ng)) * 2 + c
    nslot, nstep = (nr >> 1) & 7, nr & 1

    g3.wait_recv()
    rows = gall[...].reshape(32, 8, 128)
    pieces = []
    for v in range(4):
        total = jnp.zeros((1, 128), F32)
        for b in range(8):
            total = total + jnp.where((lane >> 4) == b, rows[8 * v + b][0:1], 0.0)
        pieces.append(total)
    dest_w = jnp.concatenate(pieces, axis=1).astype(I32)
    comes = dest_w == ndev
    stays = (dest_w < 0) & (from_w == ndev)
    rank_in = mm(one_hot(comes), before[...])
    rank_stay = mm(one_hot(stays), within[...])
    place = jnp.where(comes, rank_in + 4.0, jnp.where(stays, rank_stay, -1.0))
    order[...] = one_hot((place == nslot.astype(F32)) & ((wide & 1) == nstep))

    table = jnp.zeros((1, 128), F32)
    l_dg, l_df, l_sc = lane >> 5, (lane >> 3) & 3, (lane >> 2) & 1
    for sc in range(2):
        for a in range(4):
            for b in range(4):
                row = rows[sc * 16 + a * 4 + b][1:2]
                swapped = sc + c - 2 * sc * c
                la = a + swapped * (b - a)
                lb = b + swapped * (a - b)
                table = table + jnp.where((l_sc == sc) & (l_dg == la) & (l_df == lb), row, 0.0)
    table = table.astype(I32)
    tr = iota((32, 128), 0)
    tdg, tcore, tk = tr >> 3, (tr >> 2) & 1, tr & 3
    tl = iota((32, 128), 1)
    tg = (g + tdg) & 3
    tdev = ((f + c * (tg - f)) * 4 + tg + c * (f - tg)) * 2 + tcore
    hit = (table == tdev) & (tl < 32)
    nth = mm(one_hot(hit), earlier[...])
    pick = jnp.sum(jnp.where(hit & (nth == tk.astype(F32)), tl, 0), axis=1, keepdims=True)
    ur = iota((8, 128), 0)
    ucore, uj = ur >> 2, ur & 3
    udev = ((f + c * (g - f)) * 4 + g + c * (f - g)) * 2 + ucore
    own = table == udev
    spot = (lane >> 5) * 8 + ucore * 4 + mm(one_hot(own), earlier[...]).astype(I32)
    turn_in = mm(one_hot(own), lower[...])
    last = jnp.sum(jnp.where(own & (turn_in == uj.astype(F32)), spot, 0), axis=1, keepdims=True)
    tabv[0:32] = jnp.broadcast_to(pick, (32, 128))
    tabv[32:40] = jnp.broadcast_to(last, (8, 128))
    tcopy = pltpu.make_async_copy(tabv, tabs, lsem.at[4])
    tcopy.start()

    turn_corner(1)

    loads[2].wait()
    w0.wait_recv()
    def leg(j):
        return pltpu.make_async_remote_copy(
            src_ref=sel.at[j - 1], dst_ref=fin.at[j], send_sem=cs.at[3 + j], recv_sem=cr.at[3 + j],
            device_id=on_g(j), device_id_type=MESH,
        )

    def select_rows(legs):
        for j in legs:
            for i in range(8):
                which = tabs[j * 8 + i, 0]
                chosen = cand[which >> 3, (which >> 2) & 1, which & 3]
                if j:
                    sel[j - 1, i] = chosen
                else:
                    fin[0, i] = chosen
            if j:
                leg(j).start()

    tcopy.wait()
    for k in (1, 2, 3):
        for sc in range(2):
            arrived(k, sc).wait_recv()
    select_rows((2, 1, 3, 0))

    swaps = []
    for j in (0, 1, 3, 2):
        if j:
            for grp in range(2):
                for k in range(4):
                    l2[grp, k, j].wait_recv()
        block = in2[j].reshape(256, LAT)
        for h in range(4):
            value = mm(block, wuv[h]).reshape(8, 4, 8, VD)[:, h].reshape(64, VD)
            vals[c, pl.ds(64 * j, 64), pl.ds(VD * h, VD)] = value.astype(BF)
        swaps.append(
            send(vals.at[c, pl.ds(64 * j, 64)], vals.at[c, pl.ds(64 * j, 64)], sv.at[j], rv.at[j], sibling)
        )

    ours = pl.ds(pl.multiple_of(256 * c, 256), 256)
    others = pl.ds(pl.multiple_of(256 * (1 - c), 256), 256)
    kept_rows = mm(order[:, ours], vals[c])
    for copy in swaps:
        copy.wait_recv()
    flat[...] = (kept_rows + mm(order[:, others], vals[1 - c])).astype(BF)
    loads[3].wait()
    w1.wait_recv()

    f1, f2, f3 = (f + 1) % 4, (f + 2) % 4, (f + 3) % 4
    h1, h2, h3 = (g + 1) % 4, (g + 2) % 4, (g + 3) % 4
    low, high = pl.ds(0, 32), pl.ds(32, 32)

    def rs(s, i, src, dst, device):
        return pltpu.make_async_remote_copy(
            src_ref=src, dst_ref=dst, send_sem=srs.at[s, i], recv_sem=rrs.at[s, i],
            device_id=device, device_id_type=MESH,
        )

    def copy_of(s, i):
        table = (
            lambda: rs(s, 0, part.at[s, f2, low], rl.at[s, 0], on_f(1)),
            lambda: rs(s, 1, part.at[s, f2, high], rl.at[s, 1], on_f(3)),
            lambda: rs(s, 2, part.at[s, f1, high], ac.at[s, 0, high], on_f(1)),
            lambda: rs(s, 3, part.at[s, f3, low], ac.at[s, 1, low], on_f(3)),
            lambda: rs(s, 4, mg.at[s, 0], ac.at[s, 0, low], on_f(1)),
            lambda: rs(s, 5, mg.at[s, 1], ac.at[s, 1, high], on_f(3)),
            lambda: rs(s, 6, p2.at[s, h1], ac2.at[s, 0], on_g(1)),
            lambda: rs(s, 7, p2.at[s, h2], ac2.at[s, 1], on_g(2)),
            lambda: rs(s, 8, p2.at[s, h3], ac2.at[s, 2], on_g(3)),
        )
        return table[i]()

    c3 = pltpu.make_async_remote_copy(
        src_ref=swp, dst_ref=swr, send_sem=cs.at[7], recv_sem=cr.at[7],
        device_id=sibling, device_id_type=MESH,
    )
    def place_rows():
        for j in (1, 2, 3):
            leg(j).wait_recv()
        for j in range(MOVE):
            there = tabs[32 + (1 - c) * 4 + j, 0]
            here = tabs[32 + c * 4 + j, 0]
            swp[j] = fin[there >> 3, there & 7]
            nc_v[MOVE + j, pl.ds(mine, 32)] = fin[here >> 3, here & 7]
        c3.start()

    def store_rows():
        c3.wait_recv()
        for j in range(MOVE):
            nc_v[MOVE + j, pl.ds(theirs, 32)] = swr[j]

    def step(t, carry):

        @pl.when(t < SUBS)
        def _():
            s = t
            cols = pl.ds(pl.multiple_of(s * SUB, SUB), SUB)
            part[s] = mm(flat[...], wout[:, cols]).astype(BF).reshape(4, 64, SUB)
            for i in range(4):
                copy_of(s, i).start()

        @pl.when((t >= AT[1]) & (t < SUBS + AT[1]))
        def _():
            s = t - AT[1]
            copy_of(s, 0).wait_recv()
            mg[s, 0] = (part[s, f1, low].astype(F32) + rl[s, 0].astype(F32)).astype(BF)
            copy_of(s, 4).start()
            copy_of(s, 1).wait_recv()
            mg[s, 1] = (part[s, f3, high].astype(F32) + rl[s, 1].astype(F32)).astype(BF)
            copy_of(s, 5).start()

        @pl.when((t >= AT[2]) & (t < SUBS + AT[2]))
        def _():
            s = t - AT[2]
            for i in (2, 3, 4, 5):
                copy_of(s, i).wait_recv()
            whole = part[s, f].astype(F32) + ac[s, 0].astype(F32) + ac[s, 1].astype(F32)
            p2[s] = whole.astype(BF).reshape(4, 16, SUB)
            for i in (7, 6, 8):
                copy_of(s, i).start()

        @pl.when(t >= AT[3])
        def _():
            s = t - AT[3]
            for i in (6, 7, 8):
                copy_of(s, i).wait_recv()
            whole = p2[s, g].astype(F32)
            for i in range(3):
                whole = whole + ac2[s, i].astype(F32)
            cols = pl.ds(pl.multiple_of(s * SUB, SUB), SUB)
            att_v[:, :, cols] = whole.reshape(ROWS, 2, SUB).astype(BF)

        pl.when(t == POINT)(place_rows)
        pl.when(t == POINT + 2)(store_rows)
        return carry

    lax.fori_loop(0, SUBS + AT[3], step, 0)

    for copy in g1 + g2 + [g3, c0, w0, w1] + c1 + [leg(1), leg(2), leg(3)] + swaps + [c3]:
        copy.wait_send()
    for copy in list(l1.values()) + list(l2.values()):
        copy.wait_send()

    def drain(s, carry):
        for i in range(9):
            copy_of(s, i).wait_send()
        return carry

    lax.fori_loop(0, SUBS, drain, 0)


def per_device(cache, lengths, queries, fresh, w_uv, w_out, outgoing, targets):
    hbm = pl.BlockSpec(memory_space=pltpu.HBM)
    dma = pltpu.SemaphoreType.DMA
    scratch = [
        pltpu.SMEM((ROWS,), I32),
        pltpu.SMEM((MOVE,), I32),
        pltpu.SMEM((MOVE,), I32),
        pltpu.VMEM((ROWS, 2, ENT), BF),
        pltpu.VMEM((512, 512), BF),
        pltpu.VMEM((512, 512), BF),
        pltpu.VMEM((512, 512), BF),
        pltpu.VMEM((128, 128), BF),
        pltpu.VMEM((128, 128), BF),
        pltpu.VMEM((256, 512), BF),
        pltpu.VMEM((256, 512), BF),
        pltpu.VMEM((ROWS, CAP, ENT), BF),
        pltpu.VMEM((ROWS, 128, ENT), BF),
        pltpu.VMEM((4, LAT, VD), BF),
        pltpu.VMEM((512, D), BF),
        pltpu.VMEM((2, 4, 4, 32, LAT), BF),
        pltpu.VMEM((2, 4, 4, 32, LAT), BF),
        pltpu.VMEM((4, 4, 2, 32, LAT), BF),
        pltpu.VMEM((2, 256, 512), BF),
        pltpu.VMEM((2, 4, 4, 8, 128), F32),
        pltpu.VMEM((SUBS, 4, 64, SUB), BF),
        pltpu.VMEM((SUBS, 2, 32, SUB), BF),
        pltpu.VMEM((SUBS, 2, 32, SUB), BF),
        pltpu.VMEM((SUBS, 2, 64, SUB), BF),
        pltpu.VMEM((SUBS, 4, 16, SUB), BF),
        pltpu.VMEM((SUBS, 3, 16, SUB), BF),
        pltpu.VMEM((4, 2, MOVE, 32, ENT), BF),
        pltpu.VMEM((MOVE, 32, ENT), BF),
        pltpu.VMEM((3, 8, 32, ENT), BF),
        pltpu.VMEM((4, 8, 32, ENT), BF),
        pltpu.VMEM((MOVE, 32, ENT), BF),
        pltpu.VMEM((MOVE, 32, ENT), BF),
        pltpu.VMEM((40, 128), I32),
        pltpu.SMEM((40, 128), I32),
        dma((10,)),
        dma((7,)), dma((7,)),
        dma((2,)), dma((2,)),
        dma((2, 3)), dma((2, 3)),
        dma((2, 4, 3)), dma((2, 4, 3)),
        dma((4,)), dma((4,)),
        dma((SUBS, 9)), dma((SUBS, 9)),
        dma((8,)), dma((8,)),
        dma((3, 2)), dma((3, 2)),
    ]
    operands = (lengths, outgoing, targets, fresh, cache, queries.reshape(ROWS, 128, ENT), w_uv, w_out)
    new_cache, attended = pl.pallas_call(
        kernel,
        out_shape=(
            pltpu.VMEM((ROWS, CAP, ENT), BF),
            pltpu.VMEM((ROWS, 2, D), BF),
        ),
        in_specs=[hbm] * 8,
        out_specs=(pl.BlockSpec(memory_space=pltpu.VMEM), pl.BlockSpec(memory_space=pltpu.VMEM)),
        scratch_shapes=scratch,
        compiler_params=pltpu.CompilerParams(
            collective_id=0, has_side_effects=True, vmem_limit_bytes=56 * 1024 * 1024
        ),
        cost_estimate=pl.CostEstimate(flops=4 * 10**9, bytes_accessed=8 * 10**6, transcendentals=10**6),
        name="mla_decode",
    )(*[pltpu.with_memory_space_constraint(a, pltpu.HBM) for a in operands])
    return new_cache, attended


def solution(mesh):
    in_specs = (
        P(("rep", "dp"), None, None),
        P(("rep", "dp")),
        P(("rep", "dp"), None, None, None),
        P(("rep", "dp"), None, None),
        P("dp", None, None),
        P("dp", None),
        P(("rep", "dp")),
        P(("rep", "dp")),
    )
    out_specs = (P(("rep", "dp"), None, None), P(("rep", "dp"), None, None))
    return jax.shard_map(
        per_device, mesh=mesh, in_specs=in_specs, out_specs=out_specs, check_vma=False
    )
```
